256 devices in a mesh: tgt: 8 (over y, x_hi), sup: 32 (over z, x_lo, core).
Axes of the slice: x: 4 (x_hi: 2, x_lo: 2; x = x_hi * 2 + x_lo), y: 4, z: 8, core: 2. Of those that a mesh axis runs over, the one named last changes fastest.
Arguments:
- support: float32 [256, 3, 1024], P(('sup', 'tgt')), may hold values from -14 to 14
- coeffs: float32 [256, 100], P('sup'), may hold values from -1.25 to 1.25
- targets: float32 [256, 3, 1024], P(('tgt', 'sup')), may hold values from -14 to 14
- labels: float32 [256, 100], P(('tgt', 'sup')), may hold values from -5 to 5
Outputs:
- support_grad: float32 [256, 3, 1024], P(('sup', 'tgt'))
- residual: float32 [256, 100], P(('tgt', 'sup'))
The draws below stay inside these ranges and needn't reach their ends.
All inputs are finite; a program needn't handle non-finite values.
Results may differ from the reference program's by a relative error of at most 0.000064.
Values sent between devices are 32-bit elements; how exact they have to be, the bound alone decides.
A program may use at most 128 MiB of HBM per device.

```python
import math
import jax
import jax.numpy as jnp
from jax import lax

SIDE = 32
CH = 3
LABELS = 100
DEPTH = 3
SUP_DEV = 1
PIX = 1024
SUPPORTS = 256
TARGETS = 256
N_TGT = 8


prototype_count = 16


def prototype_bank(key):
    return jax.random.truncated_normal(jax.random.fold_in(key, 9001), -3.0, 3.0, (prototype_count, CH, PIX), jnp.float32)


def class_signs(key, image_count, salt_value):
    classes = jax.random.randint(jax.random.fold_in(key, salt_value), (image_count,), 0, prototype_count)
    sign_values = 2 * jax.random.randint(jax.random.fold_in(key, salt_value + 1), (image_count,), 0, 2) - 1
    return (classes, sign_values)


def mixed_images(key, image_count, salt_value):
    classes, sign_values = class_signs(key, image_count, salt_value)
    proto_bank = prototype_bank(key)
    amplitude = jax.random.uniform(jax.random.fold_in(key, salt_value + 2), (image_count,), jnp.float32, 0.7, 1.3)
    amplitude = amplitude * sign_values.astype(jnp.float32)
    noise_key = jax.random.fold_in(key, salt_value + 3)
    noise_part = jax.random.truncated_normal(noise_key, -3.0, 3.0, (image_count, CH, PIX), jnp.float32)
    images = amplitude[:, None, None] * jnp.take(proto_bank, classes, axis=0) + noise_part
    return images


def draw_support(key, part):
    return mixed_images(key, SUPPORTS, 101)


def draw_targets(key, part):
    return mixed_images(key, TARGETS, 201)


def draw_coeffs(key, part):
    classes, sign_values = class_signs(key, SUPPORTS, 101)
    pattern = jax.random.normal(jax.random.fold_in(key, 9002), (prototype_count, LABELS), jnp.float32)
    noise_key = jax.random.fold_in(key, 9003)
    noise_part = jax.random.normal(noise_key, (SUPPORTS, LABELS), jnp.float32)
    raw_coeffs = sign_values.astype(jnp.float32)[:, None] * jnp.take(pattern, classes, axis=0) + noise_part
    return 80.0 / SUPPORTS * jnp.clip(raw_coeffs, -4.0, 4.0)


def shard_levels(own_key, dims, cuts, low, high):
    def one(position, parts):
        steps = jax.random.uniform(jax.random.fold_in(jax.random.fold_in(own_key, 6), position), (parts,), jnp.float32, low / len(cuts), high / len(cuts))
        return jnp.repeat(jnp.exp(steps), dims[position] // parts).reshape((-1,) + (1,) * (len(dims) - position - 1))

    loudness = one(*cuts[0])
    for cut in cuts[1:]:
        loudness = loudness * one(*cut)
    return loudness


def normal_values(key, dims, scale, bound, split=(), held_as=jnp.bfloat16):
    result = jax.random.normal(key, dims, jnp.float32) * scale
    if len(split) > 0:
        result = shard_levels(key, dims, split, -0.22, 0.18) * result
    return jnp.clip(result, min=-bound, max=bound).astype(held_as)


def setup_inputs(seed: int = 0) -> dict:
    key_of = jax.random.split(jax.random.key(seed), 5)
    return {
        "support": draw_support(jax.random.fold_in(key_of[4], 71), 0),
        "coeffs": draw_coeffs(jax.random.fold_in(key_of[4], 71), 0),
        "targets": draw_targets(jax.random.fold_in(key_of[4], 71), 0),
        "labels": normal_values(key_of[3], (TARGETS, LABELS), 1.0, 5.0, ((0, 256),), jnp.float32),
    }


WEIGHT_VAR = 1.6
BIAS_VAR = 0.1

def spread(values):
    side_cells = values.shape[0]
    padded = jnp.pad(values, ((1, 1), (1, 1), (0, 0)))
    summed = jnp.zeros_like(values)
    for row_shift in range(3):
        for col_shift in range(3):
            summed = summed + padded[row_shift:row_shift + side_cells, col_shift:col_shift + side_cells]
    return summed / 9.0

def self_levels(images):
    image_count = images.shape[0]
    energy = lax.optimization_barrier(jnp.mean(images * images, axis=1))
    kernel_level = WEIGHT_VAR * spread(energy.T.reshape(SIDE, SIDE, image_count)) + BIAS_VAR
    levels = [kernel_level]
    for layer_idx in range(DEPTH - 1):
        activated = 2.0 / math.pi * jnp.arcsin(2.0 * kernel_level / (1.0 + 2.0 * kernel_level))
        kernel_level = WEIGHT_VAR * spread(activated) + BIAS_VAR
        levels.append(kernel_level)
    return levels

def pair_kernel(support, targets):
    sup_count = support.shape[0]
    tgt_count = targets.shape[0]
    sup_levels = self_levels(support)
    tgt_levels = self_levels(targets)
    products = jnp.einsum('scp,tcp->pst', support, targets, precision=lax.Precision.HIGHEST) / support.shape[1]
    kernel_level = WEIGHT_VAR * spread(products.reshape(SIDE, SIDE, sup_count * tgt_count)) + BIAS_VAR
    activated = kernel_level
    for layer_idx in range(DEPTH):
        sup_gain = lax.rsqrt(1.0 + 2.0 * sup_levels[layer_idx])
        tgt_gain = lax.rsqrt(1.0 + 2.0 * tgt_levels[layer_idx])
        correlation = 2.0 * kernel_level.reshape(SIDE, SIDE, sup_count, tgt_count) * sup_gain[:, :, :, None] * tgt_gain[:, :, None, :]
        activated = 2.0 / math.pi * jnp.arcsin(correlation)
        if layer_idx + 1 < DEPTH:
            kernel_level = WEIGHT_VAR * spread(activated.reshape(SIDE, SIDE, sup_count * tgt_count)) + BIAS_VAR
    return WEIGHT_VAR * lax.optimization_barrier(jnp.mean(activated, axis=(0, 1))) + BIAS_VAR

def reference(support, coeffs, targets, labels):
    block_size = SUP_DEV * N_TGT
    block_count = SUPPORTS // block_size
    blocks = support.reshape(block_count, block_size, CH, PIX)
    coeff_blocks = coeffs.reshape(block_count, block_size, LABELS)

    def block_predict(pair):
        piece, block_coeffs = pair
        theta = pair_kernel(piece, targets)
        return jnp.dot(theta.T, block_coeffs, precision=lax.Precision.HIGHEST, preferred_element_type=jnp.float32)
    predicted = lax.optimization_barrier(jnp.sum(lax.map(block_predict, (blocks, coeff_blocks)), axis=0))
    misfit = predicted - labels

    def block_gradient(pair):
        piece, block_coeffs = pair
        theta, pullback = jax.vjp(lambda images: pair_kernel(images, targets), piece)
        cotangent = jnp.dot(block_coeffs, misfit.T, precision=lax.Precision.HIGHEST, preferred_element_type=jnp.float32)
        return pullback(cotangent)[0]
    gradients = lax.map(block_gradient, (blocks, coeff_blocks))
    return (gradients.reshape(SUPPORTS, CH, PIX), misfit)
```

```python
import math

import jax
import jax.numpy as jnp
from jax import lax
from jax.experimental import pallas as pl
from jax.experimental.pallas import tpu as pltpu
from jax.sharding import PartitionSpec as P

f32 = jnp.float32
bf16 = jnp.bfloat16
MESH = pl.DeviceIdType.MESH
HIGHEST = lax.Precision.HIGHEST

WEIGHT_VAR = 1.6
BIAS_VAR = 0.1
LABELS = 100

GROUP = 16
ROWS = 24
SPREAD = WEIGHT_VAR / 9.0
PROD = SPREAD / 3.0
ALPHA = SPREAD * 2.0 / math.pi
BETA = WEIGHT_VAR / 1024.0 * 2.0 / math.pi

WIDE = (
    1.5707962162062898, -0.9999815161013006, 0.7848809620778067, -0.6609690948852064, 0.5565553788659177,
    -0.42358122423204403, 0.252084788157994, -0.0972640965051769, 0.017478656801048167,
)
NARROW = (
    1.5660394665702648, -0.9597383006319578, 0.6362998416714283, -0.3442600430796345, 0.12171201192018792,
    -0.020052988434709065,
)


def horner(w, coefs, scale):
    total = jnp.full_like(w, coefs[-1] * scale)
    for coef in coefs[-2::-1]:
        total = total * w + coef * scale
    return total


def lanes(shape):
    return lax.broadcasted_iota(jnp.int32, shape, len(shape) - 1)


def roll_lanes(x, shift):
    flat = x.reshape(-1, 128)
    return pltpu.roll(flat, shift, 1).reshape(x.shape)


def col_sum(x, masks):
    return x + roll_lanes(x, 1) * masks[0] + roll_lanes(x, 127) * masks[1]


def col_masks():
    col = lanes((1, 128)) % 32
    return (col != 0).astype(f32), (col != 31).astype(f32)


def self_chain(energy, box):
    gains, slopes = [], []
    level = box(energy) + BIAS_VAR
    for layer in range(3):
        gain = lax.rsqrt(1.0 + 2.0 * level)
        gains.append(gain)
        if layer < 2:
            square = gain * gain
            root = lax.rsqrt(1.0 + 4.0 * level)
            w = (1.0 + 4.0 * level) * root * square
            value = 2.0 * level * square * horner(w, NARROW if layer else WIDE, ALPHA)
            slopes.append((4.0 / math.pi * SPREAD) * square * root)
            level = box(value) + BIAS_VAR
    return gains, slopes


def box_natural(x, masks):
    h = col_sum(x, masks)
    lane = lanes((1, 1, 1, 128))
    zero = jnp.zeros_like(h[:, :1])
    above = roll_lanes(h, 32)
    below = roll_lanes(h, 96)
    above = jnp.where(lane < 32, jnp.concatenate([zero, above[:, :-1]], 1), above)
    below = jnp.where(lane >= 96, jnp.concatenate([below[:, 1:], zero], 1), below)
    return h + above + below


def prepare_supports(sbuf, srep, gsrep, slope_ref, masks):
    for sg in range(2):
        chans = [
            jnp.stack([sbuf[pl.ds(sg * 8 * ROWS + c * 8 + g, 8, stride=ROWS), :] for g in range(8)])[None]
            for c in range(3)
        ]
        energy = (chans[0] * chans[0] + chans[1] * chans[1] + chans[2] * chans[2]) * PROD
        gains, slopes = self_chain(energy, lambda x: box_natural(x, masks))
        for layer in range(2):
            slope_ref[layer, sg] = slopes[layer][0]
        for layer in range(3):
            slope_ref[2 + layer, sg] = -(gains[layer] * gains[layer])[0]
        lane = lanes((1, 128))
        low, even = lane < 64, (lane // 32) % 2 == 0
        for q in range(6):
            src = chans[q][0] * PROD if q < 3 else gains[q - 3][0] * 2.0
            dst = srep if q < 3 else gsrep
            turned = roll_lanes(src, 64)
            first, second = jnp.where(low, src, turned), jnp.where(low, turned, src)
            t1, t2 = roll_lanes(first, 32), roll_lanes(second, 32)
            reps = (jnp.where(even, first, t1), jnp.where(even, t1, first), jnp.where(even, second, t2), jnp.where(even, t2, second))
            for j in range(4):
                for g in range(8):
                    dst[sg, q % 3, g * 4 + j] = reps[j][g]


def prepare_targets(tbuf, tq, gt, masks):
    lane = lanes((1, 128))
    low, even = lane < 64, (lane // 32) % 2 == 0
    for tg in range(4):
        a = [tbuf[4 * tg + i] for i in range(4)]
        p = [None] * 4
        for i in range(2):
            p[i] = jnp.where(low, a[i], pltpu.roll(a[i + 2], 64, 1))
            p[i + 2] = jnp.where(low, pltpu.roll(a[i], 64, 1), a[i + 2])
        for k in range(2):
            b0 = jnp.where(even, p[2 * k], pltpu.roll(p[2 * k + 1], 32, 1))
            b1 = jnp.where(even, pltpu.roll(p[2 * k], 96, 1), p[2 * k + 1])
            for c in range(3):
                tq[2 * k, c, tg] = b0[c * 8 : c * 8 + 8]
                tq[2 * k + 1, c, tg] = b1[c * 8 : c * 8 + 8]
    x = [[tq[j, c].reshape(32, 128) for j in range(4)] for c in range(3)]
    energy = [(x[0][j] * x[0][j] + x[1][j] * x[1][j] + x[2][j] * x[2][j]) * PROD for j in range(4)]
    g = lax.broadcasted_iota(jnp.int32, (32, 128), 0) % 8
    not_first, not_last = (g != 0).astype(f32), (g != 7).astype(f32)

    def box(values):
        h = [col_sum(values[j * 32 : j * 32 + 32], masks) for j in range(4)]
        above = [pltpu.roll(h[3], 1, 0) * not_first] + h[:3]
        below = h[1:] + [pltpu.roll(h[0], 31, 0) * not_last]
        return jnp.concatenate([h[j] + above[j] + below[j] for j in range(4)], 0)

    gains, _ = self_chain(jnp.concatenate(energy, 0), box)
    for layer in range(3):
        for j in range(4):
            gt[j, layer] = gains[layer][j * 32 : j * 32 + 32].reshape(4, 8, 128)


def target_rows(ref, q, tg, first, count):
    return jnp.concatenate([ref[r % 4, q, tg, pl.ds(r // 4, 1), :][None] for r in range(first, first + count)], 0)


CHUNK = 8


def forward_unit(u, sg, tg, srep, gsrep, tq, gt, xs, rs, hbuf, thacc, masks):
    def put(k, r0, value):
        hbuf[k, pl.ds(1 + r0, CHUNK)] = col_sum(value, masks)

    def window(k, r0):
        return hbuf[k, pl.ds(r0, CHUNK)] + hbuf[k, pl.ds(r0 + 1, CHUNK)] + hbuf[k, pl.ds(r0 + 2, CHUNK)]

    for r0 in range(0, 32, CHUNK):
        rows = pl.ds(r0, CHUNK)
        prod = srep[sg, 0, rows] * target_rows(tq, 0, tg, r0, CHUNK)
        prod += srep[sg, 1, rows] * target_rows(tq, 1, tg, r0, CHUNK)
        prod += srep[sg, 2, rows] * target_rows(tq, 2, tg, r0, CHUNK)
        put(0, r0, prod)
    total = None
    for layer in range(3):
        for r0 in range(0, 32, CHUNK):
            rows = pl.ds(r0, CHUNK)
            level = window(layer, r0) + BIAS_VAR
            x = level * gsrep[sg, layer, rows] * target_rows(gt, layer, tg, r0, CHUNK)
            rest = 1.0 - x * x
            root = lax.rsqrt(rest)
            xs[u, layer, rows] = x
            rs[u, layer, rows] = root
            value = x * horner(rest * root, NARROW if layer else WIDE, ALPHA if layer < 2 else BETA)
            if layer < 2:
                put(layer + 1, r0, value)
            else:
                part = jnp.sum(value, axis=0)
                total = part if total is None else total + part
    thacc[u] = total


def backward_unit(u, sg, tg, gsrep, gt, xs, rs, vs, us, hbuf, masks):
    for layer in (2, 1, 0):
        for r0 in range(0, 32, CHUNK):
            rows = pl.ds(r0, CHUNK)
            d = rs[u, layer, rows]
            if layer < 2:
                k = 2 - layer - 1
                d = d * (hbuf[k, pl.ds(r0, CHUNK)] + hbuf[k, pl.ds(r0 + 1, CHUNK)] + hbuf[k, pl.ds(r0 + 2, CHUNK)])
            vs[u, layer, rows] = d * xs[u, layer, rows]
            d = d * gsrep[sg, layer, rows] * target_rows(gt, layer, tg, r0, CHUNK)
            hbuf[2 - layer, pl.ds(1 + r0, CHUNK)] = col_sum(d, masks)
    for r0 in range(0, 32, CHUNK):
        us[u, pl.ds(r0, CHUNK)] = (
            hbuf[2, pl.ds(r0, CHUNK)] + hbuf[2, pl.ds(r0 + 1, CHUNK)] + hbuf[2, pl.ds(r0 + 2, CHUNK)]
        )


def fold_rows(r):
    lane = lanes((1, 128))
    low, even = lane < 64, (lane // 32) % 2 == 0
    y = [
        jnp.where(low, r[k], r[k + 2]) + roll_lanes(jnp.where(low, r[k + 2], r[k]), 64)
        for k in range(2)
    ]
    other = jnp.where(even, y[1], y[0])
    return jnp.where(even, y[0], y[1]) + jnp.where(even, roll_lanes(other, 96), roll_lanes(other, 32))


def contract_rows(sg, g, cot, tq, vs, us, nat):
    acc = [[None] * 4 for _ in range(6)]
    for tg in range(4):
        u = tg * 2 + sg
        weight = cot[u]
        for j in range(4):
            w = us[u, g * 4 + j] * weight
            terms = [w * tq[j, c, tg, pl.ds(g, 1), :] for c in range(3)]
            terms += [vs[u, layer, g * 4 + j] * weight for layer in range(3)]
            for q in range(6):
                acc[q][j] = terms[q] if tg == 0 else acc[q][j] + terms[q]
    for q in range(6):
        nat[sg, q, g] = fold_rows(acc[q])


def finish_supports(sg, nat, sbuf, slope_ref, gout, masks):
    def box(x):
        return box_natural(x[None], masks)[0]

    scale = (BETA * ALPHA * ALPHA, BETA * ALPHA, BETA)
    parts = [nat[sg, 3 + layer] * slope_ref[2 + layer, sg] * scale[layer] for layer in range(3)]
    d2 = parts[1] + box(parts[2]) * slope_ref[1, sg]
    d1 = parts[0] + box(d2) * slope_ref[0, sg]
    energy = box(d1) * (2.0 * PROD)
    for c in range(3):
        for g in range(8):
            at = pl.ds(sg * 8 * ROWS + c * 8 + g, 8, stride=ROWS)
            gout[at, :] = nat[sg, c, g] * (BETA * ALPHA * ALPHA * PROD) + energy[g] * sbuf[at, :]


def split_dot(x, ones):
    high = x.astype(bf16)
    rest = x - high.astype(f32)
    middle = rest.astype(bf16)
    low = (rest - middle.astype(f32)).astype(bf16)
    dot = lambda part: jnp.dot(part, ones, preferred_element_type=f32)
    return dot(high) + dot(middle) + dot(low)


def kernel(
    sup_in, coef_in, tgt_in, lab_in, out_ref, res_ref,
    sin, cin, tin, lin, sbuf, tbuf, meta, thall, gout, gbuf,
    srep, gsrep, slope_ref, tq, gt, xs, rs, hbuf, thacc, vs, us, cot, nat, expand, gather, spreadth,
    in_sem, ssend, tsend, csend, msend, thsend, gsend, srecv, trecv, krecv, crecv, mrecv, threcv, grecv,
):
    tgt, sup = lax.axis_index("tgt"), lax.axis_index("sup")
    z, xlo, core = sup // 4, (sup // 2) % 2, sup % 2
    a, b = xlo * 8 + tgt, z * 2 + core

    def plane(k):
        other = (a + k) % GROUP
        return (other % 8, z * 4 + (other // 8) * 2 + core), other

    def line(k):
        other = (b + k) % GROUP
        return (tgt, (other // 2) * 4 + xlo * 2 + other % 2)

    loads = [
        pltpu.make_async_copy(src, dst, in_sem.at[i])
        for i, (src, dst) in enumerate(((sup_in, sin), (coef_in, cin), (tgt_in, tin), (lab_in, lin)))
    ]
    for load in loads:
        load.start()
    barrier = pltpu.get_barrier_semaphore()
    for k in range(1, GROUP):
        pl.semaphore_signal(barrier, inc=1, device_id=plane(k)[0], device_id_type=MESH)
        pl.semaphore_signal(barrier, inc=1, device_id=line(k), device_id_type=MESH)

    hbuf[...] = jnp.zeros_like(hbuf)
    source = lax.broadcasted_iota(jnp.int32, (512, 128), 0) // 32
    gather[...] = (source == lanes((512, 128)) % 16).astype(f32).astype(bf16)
    source = lax.broadcasted_iota(jnp.int32, (128, 512), 0) % 16
    expand[...] = (source == lanes((128, 512)) // 32).astype(f32).astype(bf16)
    masks = col_masks()

    for load in loads:
        load.wait()
    own = pl.multiple_of(a * ROWS, 8)
    for g in range(8):
        for c in range(3):
            sbuf[pl.ds(own + c * 8 + g, 1), :] = sin[0, c : c + 1, g * 128 : g * 128 + 128]
            tbuf[b, pl.ds(c * 8 + g, 1), :] = tin[0, c : c + 1, g * 128 : g * 128 + 128]
    fill = jnp.zeros((8, 128 - LABELS), f32)
    meta[b, pl.ds(pl.multiple_of(xlo * 8, 8), 8), :] = jnp.concatenate([cin[...], fill], 1)
    meta[b, 16:17, :] = jnp.concatenate([lin[...], fill[:1]], 1)

    pl.semaphore_wait(barrier, 2 * (GROUP - 1))

    copies = []

    def send(src, dst, send_sem, recv_sem, device):
        copy = pltpu.make_async_remote_copy(
            src_ref=src, dst_ref=dst, send_sem=send_sem, recv_sem=recv_sem, device_id=device, device_id_type=MESH
        )
        copy.start()

    def all_arrived(ref, sem):
        pltpu.make_async_copy(ref, ref, sem).wait()

    sibling = (tgt, sup + 1 - 2 * core)
    order = (1, 7, 2, 6, 3, 5, 4)
    mine = tbuf.at[b]
    slab = sbuf.at[pl.ds(own, ROWS)]
    send(mine, mine, tsend, krecv, sibling)
    for i, d in enumerate(order):
        send(mine, mine, tsend, trecv.at[d], (tgt, ((z + d) % 8) * 4 + xlo * 2 + core))
        send(slab, slab, ssend, srecv, plane(2 * i + 1)[0])
        send(slab, slab, ssend, srecv, plane(2 * i + 2)[0])
    send(slab, slab, ssend, srecv, plane(15)[0])
    block = meta.at[b, pl.ds(pl.multiple_of(xlo * 8, 8), 8)]
    send(block, block, csend, crecv, (tgt, z * 4 + (1 - xlo) * 2 + core))
    for d in order:
        slot = tbuf.at[((z + 8 - d) % 8) * 2 + core]
        all_arrived(slot, trecv.at[d])
        send(slot, slot, tsend, krecv, sibling)
    others = sbuf.at[pl.ds(0, (GROUP - 1) * ROWS)]
    all_arrived(others, srecv)
    prepare_supports(sbuf, srep, gsrep, slope_ref, masks)
    all_arrived(block, crecv)
    for k in range(1, GROUP):
        send(meta.at[b], meta.at[b], msend, mrecv, line(k))
    all_arrived(tbuf.at[pl.ds(0, 8)], krecv)
    prepare_targets(tbuf, tq, gt, masks)

    @pl.loop(0, 8)
    def _(u):
        forward_unit(u, u % 2, u // 2, srep, gsrep, tq, gt, xs, rs, hbuf, thacc, masks)

    sums = jnp.concatenate(
        [jnp.concatenate([thacc[tg * 2 + sg] for tg in range(4)], 1) for sg in range(2)], 0
    )
    theta = split_dot(sums, gather[...]) + BIAS_VAR
    pick = (lax.broadcasted_iota(jnp.int32, (8, 128), 0) == lanes((8, 128)) // 16).astype(f32)
    for sg in range(2):
        thall[b, sg : sg + 1, :] = jnp.sum(theta[sg * 8 : sg * 8 + 8] * pick, axis=0, keepdims=True)
    for k in range(1, GROUP):
        send(thall.at[b], thall.at[b], thsend, threcv, line(k))

    @pl.loop(0, 8)
    def _(u):
        backward_unit(u, u % 2, u // 2, gsrep, gt, xs, rs, vs, us, hbuf, masks)

    all_arrived(meta.at[pl.ds(0, GROUP - 1)], mrecv)
    coeffs = meta[b, 0:16, :]
    coeffs_all = jnp.concatenate([meta[k, 0:16, :] for k in range(GROUP)], 0)
    labels = jnp.concatenate([meta[k, 16:17, :] for k in range(GROUP)], 0)
    contract_last = (((1,), (1,)), ((), ()))
    gram = lax.dot_general(coeffs, coeffs_all, contract_last, precision=HIGHEST, preferred_element_type=f32)
    wanted = lax.dot_general(coeffs, labels, contract_last, precision=HIGHEST, preferred_element_type=f32)
    wanted = jnp.concatenate([wanted, jnp.zeros((16, 112), f32)], 1)

    all_arrived(thall.at[pl.ds(0, GROUP - 1)], threcv)
    for k in range(GROUP):
        for sg in range(2):
            spreadth[pl.ds(k * 16 + sg * 8, 8), :] = thall[k, sg : sg + 1, :] * pick
    values = jnp.dot(gram, spreadth[...], precision=HIGHEST, preferred_element_type=f32) - wanted
    weights = split_dot(values, expand[...])
    for sg in range(2):
        for tg in range(4):
            cot[tg * 2 + sg] = weights[sg * 8 : sg * 8 + 8, tg * 128 : tg * 128 + 128]

    for sg in range(2):

        @pl.loop(0, 8)
        def _(g):
            contract_rows(sg, g, cot, tq, vs, us, nat)

        finish_supports(sg, nat, sbuf, slope_ref, gout, masks)
        for k in range(8):
            to = sg * 8 + (tgt + k) % 8
            if k == 0:

                @pl.when(sg != xlo)
                def _():
                    piece = gout.at[pl.ds(pl.multiple_of(to * ROWS, 8), ROWS)]
                    send(piece, gbuf.at[a], gsend, grecv, (tgt, z * 4 + sg * 2 + core))
            else:
                piece = gout.at[pl.ds(pl.multiple_of(to * ROWS, 8), ROWS)]
                send(piece, gbuf.at[a], gsend, grecv, ((tgt + k) % 8, z * 4 + sg * 2 + core))

    column = (lanes((1, 128)) % 16 == b).astype(f32)
    picked = jnp.sum(spreadth[...] * column, axis=1, keepdims=True)
    predicted = jnp.sum(picked * coeffs_all, axis=0, keepdims=True)
    res_ref[...] = (predicted - meta[b, 16:17, :])[:, :LABELS]

    gbuf[a] = gout[pl.ds(own, ROWS), :]
    all_arrived(gbuf.at[pl.ds(0, GROUP - 1)], grecv)
    total = gbuf[0]
    for k in range(1, GROUP):
        total = total + gbuf[k]
    out_ref[...] = total

    all_arrived(others, ssend)
    all_arrived(tbuf.at[pl.ds(0, GROUP - 1)], tsend)
    all_arrived(block, csend)
    all_arrived(meta.at[pl.ds(0, GROUP - 1)], msend)
    all_arrived(thall.at[pl.ds(0, GROUP - 1)], thsend)
    all_arrived(gbuf.at[pl.ds(0, GROUP - 1)], gsend)


def local(support, coeffs, targets, labels):
    vmem = lambda *shape: pltpu.VMEM(shape, f32)
    dma = pltpu.SemaphoreType.DMA
    grad, residual = pl.pallas_call(
        kernel,
        out_shape=(jax.ShapeDtypeStruct((ROWS, 128), f32), jax.ShapeDtypeStruct((1, LABELS), f32)),
        in_specs=[pl.BlockSpec(memory_space=pl.ANY)] * 4,
        out_specs=(pl.BlockSpec(memory_space=pltpu.VMEM), pl.BlockSpec(memory_space=pltpu.VMEM)),
        scratch_shapes=[
            vmem(1, 3, 1024), vmem(8, LABELS), vmem(1, 3, 1024), vmem(1, LABELS),
            vmem(GROUP * ROWS, 128), vmem(GROUP, ROWS, 128), vmem(GROUP, 17, 128), vmem(GROUP, 2, 128),
            vmem(GROUP * ROWS, 128), vmem(GROUP, ROWS, 128),
            vmem(2, 3, 32, 8, 128), vmem(2, 3, 32, 8, 128), vmem(5, 2, 8, 8, 128),
            vmem(4, 3, 4, 8, 128), vmem(4, 3, 4, 8, 128),
            vmem(8, 3, 32, 8, 128), vmem(8, 3, 32, 8, 128), vmem(3, 34, 8, 128), vmem(8, 8, 128),
            vmem(8, 3, 32, 8, 128), vmem(8, 32, 8, 128), vmem(8, 8, 128), vmem(2, 6, 8, 8, 128),
            pltpu.VMEM((128, 512), bf16), pltpu.VMEM((512, 128), bf16), vmem(256, 128),
            dma((4,)), dma, dma, dma, dma, dma, dma, dma, dma((8,)), dma, dma, dma, dma, dma,
        ],
        compiler_params=pltpu.CompilerParams(
            collective_id=0, has_side_effects=True, vmem_limit_bytes=48 * 1024 * 1024
        ),
    )(support, coeffs, targets, labels)
    return grad.reshape(1, 3, 1024), residual


def solution(mesh):
    return jax.shard_map(
        local,
        mesh=mesh,
        in_specs=(
            P(("sup", "tgt"), None, None),
            P("sup", None),
            P(("tgt", "sup"), None, None),
            P(("tgt", "sup"), None),
        ),
        out_specs=(P(("sup", "tgt"), None, None), P(("tgt", "sup"), None)),
        check_vma=False,
    )
```

```python
import math

import jax
import jax.numpy as jnp
from jax import lax
from jax.experimental import pallas as pl
from jax.experimental.pallas import tpu as pltpu
from jax.sharding import PartitionSpec as P

f32 = jnp.float32
bf16 = jnp.bfloat16
MESH = pl.DeviceIdType.MESH
HIGHEST = lax.Precision.HIGHEST

WEIGHT_VAR = 1.6
BIAS_VAR = 0.1
LABELS = 100

GROUP = 16
ROWS = 24
SPREAD = WEIGHT_VAR / 9.0
PROD = SPREAD / 3.0
ALPHA = SPREAD * 2.0 / math.pi
BETA = WEIGHT_VAR / 1024.0 * 2.0 / math.pi

WIDE = (
    1.5707962162062898, -0.9999815161013006, 0.7848809620778067, -0.6609690948852064, 0.5565553788659177,
    -0.42358122423204403, 0.252084788157994, -0.0972640965051769, 0.017478656801048167,
)
NARROW = (
    1.5660394665702648, -0.9597383006319578, 0.6362998416714283, -0.3442600430796345, 0.12171201192018792,
    -0.020052988434709065,
)


def horner(w, coefs, scale):
    total = jnp.full_like(w, coefs[-1] * scale)
    for coef in coefs[-2::-1]:
        total = total * w + coef * scale
    return total


def lanes(shape):
    return lax.broadcasted_iota(jnp.int32, shape, len(shape) - 1)


def roll_lanes(x, shift):
    flat = x.reshape(-1, 128)
    return pltpu.roll(flat, shift, 1).reshape(x.shape)


def col_sum(x, masks):
    return x + roll_lanes(x, 1) * masks[0] + roll_lanes(x, 127) * masks[1]


def col_masks():
    col = lanes((1, 128)) % 32
    return (col != 0).astype(f32), (col != 31).astype(f32)


def self_chain(energy, box):
    gains, slopes = [], []
    level = box(energy) + BIAS_VAR
    for layer in range(3):
        gain = lax.rsqrt(1.0 + 2.0 * level)
        gains.append(gain)
        if layer < 2:
            square = gain * gain
            root = lax.rsqrt(1.0 + 4.0 * level)
            w = (1.0 + 4.0 * level) * root * square
            value = 2.0 * level * square * horner(w, NARROW if layer else WIDE, ALPHA)
            slopes.append((4.0 / math.pi * SPREAD) * square * root)
            level = box(value) + BIAS_VAR
    return gains, slopes


def box_natural(x, masks):
    h = col_sum(x, masks)
    lane = lanes((1, 1, 1, 128))
    zero = jnp.zeros_like(h[:, :1])
    above = roll_lanes(h, 32)
    below = roll_lanes(h, 96)
    above = jnp.where(lane < 32, jnp.concatenate([zero, above[:, :-1]], 1), above)
    below = jnp.where(lane >= 96, jnp.concatenate([below[:, 1:], zero], 1), below)
    return h + above + below


def prepare_supports(sbuf, srep, gsrep, slope_ref, masks):
    for sg in range(2):
        chans = [
            jnp.stack([sbuf[pl.ds(sg * 8 * ROWS + c * 8 + g, 8, stride=ROWS), :] for g in range(8)])[None]
            for c in range(3)
        ]
        energy = (chans[0] * chans[0] + chans[1] * chans[1] + chans[2] * chans[2]) * PROD
        gains, slopes = self_chain(energy, lambda x: box_natural(x, masks))
        for layer in range(2):
            slope_ref[layer, sg] = slopes[layer][0]
        for layer in range(3):
            slope_ref[2 + layer, sg] = -(gains[layer] * gains[layer])[0]
        lane = lanes((1, 128))
        low, even = lane < 64, (lane // 32) % 2 == 0
        for q in range(6):
            src = chans[q][0] * PROD if q < 3 else gains[q - 3][0] * 2.0
            dst = srep if q < 3 else gsrep
            turned = roll_lanes(src, 64)
            first, second = jnp.where(low, src, turned), jnp.where(low, turned, src)
            t1, t2 = roll_lanes(first, 32), roll_lanes(second, 32)
            reps = (jnp.where(even, first, t1), jnp.where(even, t1, first), jnp.where(even, second, t2), jnp.where(even, t2, second))
            for j in range(4):
                for g in range(8):
                    dst[sg, q % 3, g * 4 + j] = reps[j][g]


def prepare_targets(half, slots, tbuf, tq, gt, masks):
    lane = lanes((1, 128))
    low, even = lane < 64, (lane // 32) % 2 == 0
    for unit in range(2):
        tg = 2 * half + unit
        a = [tbuf[slots[tg][i]] for i in range(4)]
        p = [None] * 4
        for i in range(2):
            p[i] = jnp.where(low, a[i], pltpu.roll(a[i + 2], 64, 1))
            p[i + 2] = jnp.where(low, pltpu.roll(a[i], 64, 1), a[i + 2])
        for k in range(2):
            b0 = jnp.where(even, p[2 * k], pltpu.roll(p[2 * k + 1], 32, 1))
            b1 = jnp.where(even, pltpu.roll(p[2 * k], 96, 1), p[2 * k + 1])
            for c in range(3):
                tq[2 * k, c, tg] = b0[c * 8 : c * 8 + 8]
                tq[2 * k + 1, c, tg] = b1[c * 8 : c * 8 + 8]
    x = [[tq[j, c, 2 * half : 2 * half + 2].reshape(16, 128) for j in range(4)] for c in range(3)]
    energy = [(x[0][j] * x[0][j] + x[1][j] * x[1][j] + x[2][j] * x[2][j]) * PROD for j in range(4)]
    g = lax.broadcasted_iota(jnp.int32, (16, 128), 0) % 8
    not_first, not_last = (g != 0).astype(f32), (g != 7).astype(f32)

    def box(values):
        flat = col_sum(values, masks)
        h = [flat[j * 16 : j * 16 + 16] for j in range(4)]
        above = [pltpu.roll(h[3], 1, 0) * not_first] + h[:3]
        below = h[1:] + [pltpu.roll(h[0], 15, 0) * not_last]
        return jnp.concatenate([h[j] + above[j] + below[j] for j in range(4)], 0)

    gains, _ = self_chain(jnp.concatenate(energy, 0), box)
    for layer in range(3):
        for j in range(4):
            gt[j, layer, 2 * half : 2 * half + 2] = gains[layer][j * 16 : j * 16 + 16].reshape(2, 8, 128)


def target_rows(ref, q, tg, first, count):
    return jnp.concatenate([ref[r % 4, q, tg, pl.ds(r // 4, 1), :][None] for r in range(first, first + count)], 0)


CHUNK = 16


def forward_unit(u, sg, tg, srep, gsrep, tq, gt, xs, rs, hbuf, thacc, masks):
    def put(k, r0, value):
        hbuf[k, pl.ds(1 + r0, CHUNK)] = col_sum(value, masks)

    def window(k, r0):
        return hbuf[k, pl.ds(r0, CHUNK)] + hbuf[k, pl.ds(r0 + 1, CHUNK)] + hbuf[k, pl.ds(r0 + 2, CHUNK)]

    for r0 in range(0, 32, CHUNK):
        rows = pl.ds(r0, CHUNK)
        prod = srep[sg, 0, rows] * target_rows(tq, 0, tg, r0, CHUNK)
        prod += srep[sg, 1, rows] * target_rows(tq, 1, tg, r0, CHUNK)
        prod += srep[sg, 2, rows] * target_rows(tq, 2, tg, r0, CHUNK)
        put(0, r0, prod)
    total = None
    for layer in range(3):
        for r0 in range(0, 32, CHUNK):
            rows = pl.ds(r0, CHUNK)
            level = window(layer, r0) + BIAS_VAR
            x = level * gsrep[sg, layer, rows] * target_rows(gt, layer, tg, r0, CHUNK)
            rest = 1.0 - x * x
            root = lax.rsqrt(rest)
            xs[u, layer, rows] = x
            rs[u, layer, rows] = root
            value = x * horner(rest * root, NARROW if layer else WIDE, ALPHA if layer < 2 else BETA)
            if layer < 2:
                put(layer + 1, r0, value)
            else:
                part = jnp.sum(value, axis=0)
                total = part if total is None else total + part
    thacc[u] = total


def backward_unit(u, sg, tg, gsrep, gt, xs, rs, vs, us, hbuf, masks):
    for layer in (2, 1, 0):
        for r0 in range(0, 32, CHUNK):
            rows = pl.ds(r0, CHUNK)
            d = rs[u, layer, rows]
            if layer < 2:
                k = 2 - layer - 1
                d = d * (hbuf[k, pl.ds(r0, CHUNK)] + hbuf[k, pl.ds(r0 + 1, CHUNK)] + hbuf[k, pl.ds(r0 + 2, CHUNK)])
            vs[u, layer, rows] = d * xs[u, layer, rows]
            d = d * gsrep[sg, layer, rows] * target_rows(gt, layer, tg, r0, CHUNK)
            hbuf[2 - layer, pl.ds(1 + r0, CHUNK)] = col_sum(d, masks)
    for r0 in range(0, 32, CHUNK):
        us[u, pl.ds(r0, CHUNK)] = (
            hbuf[2, pl.ds(r0, CHUNK)] + hbuf[2, pl.ds(r0 + 1, CHUNK)] + hbuf[2, pl.ds(r0 + 2, CHUNK)]
        )


def fold_rows(rows):
    block = lanes((1, 1, 128)) // 32
    r = (rows[1], rows[2], rows[3], rows[0])
    low, middle, odd = block < 2, (block == 1) | (block == 2), block % 2 == 1
    y0 = jnp.where(low, r[0], r[2]) + roll_lanes(jnp.where(low, r[2], r[0]), 64)
    y1 = jnp.where(middle, r[1], r[3]) + roll_lanes(jnp.where(middle, r[3], r[1]), 64)
    return jnp.where(odd, y0, y1) + roll_lanes(jnp.where(odd, y1, y0), 32)


def contract_rows(sg, cot, tq, vs, us, accs, nat):
    @pl.loop(0, 8)
    def _(g):
        for j in range(4):
            acc = [None] * 6
            for tg in range(4):
                u = tg * 2 + sg
                weight = cot[u]
                w = us[u, g * 4 + j] * weight
                terms = [w * tq[j, c, tg, pl.ds(g, 1), :] for c in range(3)]
                terms += [vs[u, layer, g * 4 + j] * weight for layer in range(3)]
                acc = [term if tg == 0 else old + term for old, term in zip(acc, terms)]
            for q in range(6):
                accs[q, j, g] = acc[q]

    for q in range(6):
        nat[sg, q] = fold_rows([accs[q, j] for j in range(4)])


def finish_supports(sg, nat, sbuf, slope_ref, gout, masks):
    def box(x):
        return box_natural(x[None], masks)[0]

    scale = (BETA * ALPHA * ALPHA, BETA * ALPHA, BETA)
    parts = [nat[sg, 3 + layer] * slope_ref[2 + layer, sg] * scale[layer] for layer in range(3)]
    d2 = parts[1] + box(parts[2]) * slope_ref[1, sg]
    d1 = parts[0] + box(d2) * slope_ref[0, sg]
    energy = box(d1) * (2.0 * PROD)
    for c in range(3):
        for g in range(8):
            at = pl.ds(sg * 8 * ROWS + c * 8 + g, 8, stride=ROWS)
            gout[at, :] = nat[sg, c, g] * (BETA * ALPHA * ALPHA * PROD) + energy[g] * sbuf[at, :]


def split_dot(x, ones):
    high = x.astype(bf16)
    rest = x - high.astype(f32)
    middle = rest.astype(bf16)
    low = (rest - middle.astype(f32)).astype(bf16)
    dot = lambda part: jnp.dot(part, ones, preferred_element_type=f32)
    return dot(high) + dot(middle) + dot(low)


def kernel(
    sup_in, coef_in, tgt_in, lab_in, out_ref, res_ref,
    cin, lin, sbuf, tbuf, meta, thall, gout, gbuf,
    srep, gsrep, slope_ref, tq, gt, xs, rs, hbuf, thacc, vs, us, cot, accs, nat, expand, gather, spreadth,
    in_sem, ssend, tsend, csend, msend, thsend, gsend, srecv, trecv, krecv, crecv, mrecv, threcv, grecv,
):
    tgt, sup = lax.axis_index("tgt"), lax.axis_index("sup")
    z, xlo, core = sup // 4, (sup // 2) % 2, sup % 2
    a, b = xlo * 8 + tgt, z * 2 + core

    def plane(k):
        other = (a + k) % GROUP
        return (other % 8, z * 4 + (other // 8) * 2 + core), other

    def line(k):
        other = (b + k) % GROUP
        return (tgt, (other // 2) * 4 + xlo * 2 + other % 2)

    barrier = pltpu.get_barrier_semaphore()
    for k in range(1, GROUP):
        pl.semaphore_signal(barrier, inc=1, device_id=plane(k)[0], device_id_type=MESH)
        pl.semaphore_signal(barrier, inc=1, device_id=line(k), device_id_type=MESH)
    own = pl.multiple_of(a * ROWS, 8)
    mine = tbuf.at[b]
    slab = sbuf.at[pl.ds(own, ROWS)]
    loads = [
        pltpu.make_async_copy(src, dst, in_sem.at[i])
        for i, (src, dst) in enumerate(((sup_in, slab), (tgt_in, mine), (coef_in, cin), (lab_in, lin)))
    ]
    for load in loads:
        load.start()

    hbuf[...] = jnp.zeros_like(hbuf)
    slots = [[((z + step + 8) % 8) * 2 + i for step in (-k, k + 1) for i in range(2)] for k in range(4)]

    def slot_of(place):
        unit, i = place // 4, place % 4
        return ((jnp.where(i < 2, -unit, unit + 1) + z + 8) % 8) * 2 + i % 2

    place = lax.broadcasted_iota(jnp.int32, (512, 128), 0) // 32
    gather[...] = (slot_of(place) == lanes((512, 128)) % 16).astype(f32).astype(bf16)
    place = lanes((128, 512)) // 32
    expand[...] = (slot_of(place) == lax.broadcasted_iota(jnp.int32, (128, 512), 0) % 16).astype(f32).astype(bf16)
    masks = col_masks()

    for load in loads:
        load.wait()
    fill = jnp.zeros((8, 128 - LABELS), f32)
    meta[b, pl.ds(pl.multiple_of(xlo * 8, 8), 8), :] = jnp.concatenate([cin[...], fill], 1)
    meta[b, 16:17, :] = jnp.concatenate([lin[...], fill[:1]], 1)

    pl.semaphore_wait(barrier, 2 * (GROUP - 1))

    def send(src, dst, send_sem, recv_sem, device):
        copy = pltpu.make_async_remote_copy(
            src_ref=src, dst_ref=dst, send_sem=send_sem, recv_sem=recv_sem, device_id=device, device_id_type=MESH
        )
        copy.start()

    def all_arrived(ref, sem):
        pltpu.make_async_copy(ref, ref, sem).wait()

    sibling = (tgt, sup + 1 - 2 * core)
    order = (7, 1, 6, 2, 5, 3, 4)
    send(mine, mine, tsend, krecv.at[0], sibling)
    for i, d in enumerate(order):
        send(mine, mine, tsend, trecv.at[d], (tgt, ((z + d) % 8) * 4 + xlo * 2 + core))
        send(slab, slab, ssend, srecv, plane(2 * i + 1)[0])
        send(slab, slab, ssend, srecv, plane(2 * i + 2)[0])
    send(slab, slab, ssend, srecv, plane(15)[0])
    block = meta.at[b, pl.ds(pl.multiple_of(xlo * 8, 8), 8)]
    send(block, block, csend, crecv, (tgt, z * 4 + (1 - xlo) * 2 + core))

    def pass_on(steps, half):
        for d in steps:
            slot = tbuf.at[((z + 8 - d) % 8) * 2 + core]
            all_arrived(slot, trecv.at[d])
            send(slot, slot, tsend, krecv.at[half], sibling)

    def forward_half(half):
        @pl.loop(0, 4)
        def _(i):
            sg, tg = i % 2, 2 * half + i // 2
            forward_unit(tg * 2 + sg, sg, tg, srep, gsrep, tq, gt, xs, rs, hbuf, thacc, masks)

    pass_on(order[:3], 0)
    all_arrived(tbuf.at[pl.ds(0, 4)], krecv.at[0])
    prepare_targets(0, slots, tbuf, tq, gt, masks)
    pass_on(order[3:], 1)
    others = sbuf.at[pl.ds(0, (GROUP - 1) * ROWS)]
    all_arrived(others, srecv)
    all_arrived(block, crecv)
    for k in range(1, GROUP):
        send(meta.at[b], meta.at[b], msend, mrecv, line(k))
    prepare_supports(sbuf, srep, gsrep, slope_ref, masks)
    forward_half(0)
    all_arrived(tbuf.at[pl.ds(0, 4)], krecv.at[1])
    prepare_targets(1, slots, tbuf, tq, gt, masks)
    forward_half(1)

    sums = jnp.concatenate(
        [jnp.concatenate([thacc[tg * 2 + sg] for tg in range(4)], 1) for sg in range(2)], 0
    )
    theta = split_dot(sums, gather[...]) + BIAS_VAR
    pick = (lax.broadcasted_iota(jnp.int32, (8, 128), 0) == lanes((8, 128)) // 16).astype(f32)
    for sg in range(2):
        thall[b, sg : sg + 1, :] = jnp.sum(theta[sg * 8 : sg * 8 + 8] * pick, axis=0, keepdims=True)
    for k in range(1, GROUP):
        send(thall.at[b], thall.at[b], thsend, threcv, line(k))

    @pl.loop(0, 8)
    def _(u):
        backward_unit(u, u % 2, u // 2, gsrep, gt, xs, rs, vs, us, hbuf, masks)

    all_arrived(meta.at[pl.ds(0, GROUP - 1)], mrecv)
    coeffs = meta[b, 0:16, :]
    coeffs_all = jnp.concatenate([meta[k, 0:16, :] for k in range(GROUP)], 0)
    labels = jnp.concatenate([meta[k, 16:17, :] for k in range(GROUP)], 0)
    contract_last = (((1,), (1,)), ((), ()))
    gram = lax.dot_general(coeffs, coeffs_all, contract_last, precision=HIGHEST, preferred_element_type=f32)
    wanted = lax.dot_general(coeffs, labels, contract_last, precision=HIGHEST, preferred_element_type=f32)
    wanted = jnp.concatenate([wanted, jnp.zeros((16, 112), f32)], 1)

    all_arrived(thall.at[pl.ds(0, GROUP - 1)], threcv)
    for k in range(GROUP):
        for sg in range(2):
            spreadth[pl.ds(k * 16 + sg * 8, 8), :] = thall[k, sg : sg + 1, :] * pick
    values = jnp.dot(gram, spreadth[...], precision=HIGHEST, preferred_element_type=f32) - wanted
    weights = split_dot(values, expand[...])
    for sg in range(2):
        for tg in range(4):
            cot[tg * 2 + sg] = weights[sg * 8 : sg * 8 + 8, tg * 128 : tg * 128 + 128]

    for sg in range(2):
        contract_rows(sg, cot, tq, vs, us, accs, nat)
        finish_supports(sg, nat, sbuf, slope_ref, gout, masks)
        for k in range(8):
            to = sg * 8 + (tgt + k) % 8
            if k == 0:

                @pl.when(sg != xlo)
                def _():
                    piece = gout.at[pl.ds(pl.multiple_of(to * ROWS, 8), ROWS)]
                    send(piece, gbuf.at[a], gsend, grecv, (tgt, z * 4 + sg * 2 + core))
            else:
                piece = gout.at[pl.ds(pl.multiple_of(to * ROWS, 8), ROWS)]
                send(piece, gbuf.at[a], gsend, grecv, ((tgt + k) % 8, z * 4 + sg * 2 + core))

    column = (lanes((1, 128)) % 16 == b).astype(f32)
    picked = jnp.sum(spreadth[...] * column, axis=1, keepdims=True)
    predicted = jnp.sum(picked * coeffs_all, axis=0, keepdims=True)
    res_ref[...] = (predicted - meta[b, 16:17, :])[:, :LABELS]

    gbuf[a] = gout[pl.ds(own, ROWS), :]
    all_arrived(gbuf.at[pl.ds(0, GROUP - 1)], grecv)
    total = gbuf[0]
    for k in range(1, GROUP):
        total = total + gbuf[k]
    out_ref[...] = total

    all_arrived(others, ssend)
    all_arrived(tbuf.at[pl.ds(0, GROUP - 1)], tsend)
    all_arrived(block, csend)
    all_arrived(meta.at[pl.ds(0, GROUP - 1)], msend)
    all_arrived(thall.at[pl.ds(0, GROUP - 1)], thsend)
    all_arrived(gbuf.at[pl.ds(0, GROUP - 1)], gsend)


def write(grad_in, res_in, grad_out, res_out, sem):
    copies = [
        pltpu.make_async_copy(src, dst, sem.at[i])
        for i, (src, dst) in enumerate(((grad_in, grad_out), (res_in, res_out)))
    ]
    for copy in copies:
        copy.start()
    for copy in copies:
        copy.wait()


def local(support, coeffs, targets, labels):
    vmem = lambda *shape: pltpu.VMEM(shape, f32)
    dma = pltpu.SemaphoreType.DMA
    grad, residual = pl.pallas_call(
        kernel,
        out_shape=(pltpu.VMEM((ROWS, 128), f32), pltpu.VMEM((1, LABELS), f32)),
        in_specs=[pl.BlockSpec(memory_space=pltpu.HBM)] * 4,
        out_specs=(pl.BlockSpec(memory_space=pltpu.VMEM), pl.BlockSpec(memory_space=pltpu.VMEM)),
        scratch_shapes=[
            vmem(8, LABELS), vmem(1, LABELS),
            vmem(GROUP * ROWS, 128), vmem(GROUP, ROWS, 128), vmem(GROUP, 17, 128), vmem(GROUP, 2, 128),
            vmem(GROUP * ROWS, 128), vmem(GROUP, ROWS, 128),
            vmem(2, 3, 32, 8, 128), vmem(2, 3, 32, 8, 128), vmem(5, 2, 8, 8, 128),
            vmem(4, 3, 4, 8, 128), vmem(4, 3, 4, 8, 128),
            vmem(8, 3, 32, 8, 128), vmem(8, 3, 32, 8, 128), vmem(3, 34, 8, 128), vmem(8, 8, 128),
            vmem(8, 3, 32, 8, 128), vmem(8, 32, 8, 128), vmem(8, 8, 128), vmem(6, 4, 8, 8, 128), vmem(2, 6, 8, 8, 128),
            pltpu.VMEM((128, 512), bf16), pltpu.VMEM((512, 128), bf16), vmem(256, 128),
            dma((4,)), dma, dma, dma, dma, dma, dma, dma, dma((8,)), dma((2,)), dma, dma, dma, dma,
        ],
        compiler_params=pltpu.CompilerParams(
            collective_id=0, has_side_effects=True, vmem_limit_bytes=56000 * 1024
        ),
    )(support.reshape(ROWS, 128), coeffs, targets.reshape(ROWS, 128), labels)
    grad, residual = pl.pallas_call(
        write,
        out_shape=(jax.ShapeDtypeStruct((ROWS, 128), f32), jax.ShapeDtypeStruct((1, LABELS), f32)),
        in_specs=[pl.BlockSpec(memory_space=pltpu.VMEM)] * 2,
        out_specs=(pl.BlockSpec(memory_space=pltpu.HBM), pl.BlockSpec(memory_space=pltpu.HBM)),
        scratch_shapes=[dma((2,))],
        compiler_params=pltpu.CompilerParams(vmem_limit_bytes=1024 * 1024),
    )(grad, residual)
    return grad.reshape(1, 3, 1024), residual


def solution(mesh):
    return jax.shard_map(
        local,
        mesh=mesh,
        in_specs=(
            P(("sup", "tgt"), None, None),
            P("sup", None),
            P(("tgt", "sup"), None, None),
            P(("tgt", "sup"), None),
        ),
        out_specs=(P(("sup", "tgt"), None, None), P(("tgt", "sup"), None)),
        check_vma=False,
    )
```

```python
import math

import jax
import jax.numpy as jnp
from jax import lax
from jax.experimental import pallas as pl
from jax.experimental.pallas import tpu as pltpu
from jax.sharding import PartitionSpec as P

f32 = jnp.float32
bf16 = jnp.bfloat16
MESH = pl.DeviceIdType.MESH
HIGHEST = lax.Precision.HIGHEST

WEIGHT_VAR = 1.6
BIAS_VAR = 0.1
LABELS = 100

GROUP = 16
ROWS = 24
SPREAD = WEIGHT_VAR / 9.0
PROD = SPREAD / 3.0
ALPHA = SPREAD * 2.0 / math.pi
BETA = WEIGHT_VAR / 1024.0 * 2.0 / math.pi

WIDE = (
    1.5707956460959935, -0.999909759045268, 0.7833927466035577, -0.6491778438734823, 0.5105887741390924,
    -0.3261364828462018, 0.1375277539431936, -0.027081268358035065,
)
NARROW = (1.5592713649848087, -0.9171235094499794, 0.5296910993035006, -0.21179670068297385, 0.039958000056267685)

PLANE = sorted(
    ((dx, dy) for dx in range(4) for dy in range(4) if dx or dy), key=lambda p: -min(p[0], 4 - p[0]) - min(p[1], 4 - p[1])
)
LINE = sorted(((dz, dc) for dz in range(8) for dc in range(2) if dz or dc), key=lambda p: -min(p[0], 8 - p[0]))
FAR_Z = (4, 5, 3, 6, 2, 7, 1)


def horner(w, coefs, scale):
    total = jnp.full_like(w, coefs[-1] * scale)
    for coef in coefs[-2::-1]:
        total = total * w + coef * scale
    return total


def lanes(shape):
    return lax.broadcasted_iota(jnp.int32, shape, len(shape) - 1)


def roll_lanes(x, shift):
    flat = x.reshape(-1, 128)
    return pltpu.roll(flat, shift, 1).reshape(x.shape)


def col_sum(x, masks):
    return x + roll_lanes(x, 1) * masks[0] + roll_lanes(x, 127) * masks[1]


def col_masks():
    col = lanes((1, 128)) % 32
    return (col != 0).astype(f32), (col != 31).astype(f32)


def self_chain(energy, box):
    gains, slopes = [], []
    level = box(energy) + BIAS_VAR
    for layer in range(3):
        gain = lax.rsqrt(1.0 + 2.0 * level)
        gains.append(gain)
        if layer < 2:
            square = gain * gain
            root = lax.rsqrt(1.0 + 4.0 * level)
            w = (1.0 + 4.0 * level) * root * square
            value = 2.0 * level * square * horner(w, NARROW if layer else WIDE, ALPHA)
            slopes.append((4.0 / math.pi * SPREAD) * square * root)
            level = box(value) + BIAS_VAR
    return gains, slopes


def box_natural(x, masks):
    h = col_sum(x, masks)
    lane = lanes((1, 1, 1, 128))
    zero = jnp.zeros_like(h[:, :1])
    above = roll_lanes(h, 32)
    below = roll_lanes(h, 96)
    above = jnp.where(lane < 32, jnp.concatenate([zero, above[:, :-1]], 1), above)
    below = jnp.where(lane >= 96, jnp.concatenate([below[:, 1:], zero], 1), below)
    return h + above + below


def prepare_supports(sbuf, srep, gsrep, slope_ref, masks):
    chans = [
        jnp.stack([sbuf[pl.ds(sg * 8 * ROWS + c * 8 + g, 8, stride=ROWS), :] for sg in range(2) for g in range(8)])
        for c in range(3)
    ]
    energy = (chans[0] * chans[0] + chans[1] * chans[1] + chans[2] * chans[2]) * PROD
    gains, slopes = self_chain(energy.reshape(2, 8, 8, 128), lambda x: box_natural(x, masks))
    for layer in range(2):
        slope_ref[layer] = slopes[layer]
    for layer in range(3):
        slope_ref[2 + layer] = -(gains[layer] * gains[layer])
    lane = lanes((1, 128))
    low, even = lane < 64, (lane // 32) % 2 == 0
    for q in range(6):
        src = chans[q] * PROD if q < 3 else gains[q - 3].reshape(16, 8, 128) * 2.0
        dst = srep if q < 3 else gsrep
        turned = roll_lanes(src, 64)
        first, second = jnp.where(low, src, turned), jnp.where(low, turned, src)
        t1, t2 = roll_lanes(first, 32), roll_lanes(second, 32)
        reps = (jnp.where(even, first, t1), jnp.where(even, t1, first), jnp.where(even, second, t2), jnp.where(even, t2, second))
        for j in range(4):
            for sg in range(2):
                for g in range(8):
                    dst[sg, q % 3, g * 4 + j] = reps[j][sg * 8 + g]


def prepare_targets(half, slots, tbuf, tq, gt, masks):
    lane = lanes((1, 128))
    low, even = lane < 64, (lane // 32) % 2 == 0
    for unit in range(2):
        tg = 2 * half + unit
        a = [tbuf[slots[tg][i]] for i in range(4)]
        p = [None] * 4
        for i in range(2):
            p[i] = jnp.where(low, a[i], pltpu.roll(a[i + 2], 64, 1))
            p[i + 2] = jnp.where(low, pltpu.roll(a[i], 64, 1), a[i + 2])
        for k in range(2):
            b0 = jnp.where(even, p[2 * k], pltpu.roll(p[2 * k + 1], 32, 1))
            b1 = jnp.where(even, pltpu.roll(p[2 * k], 96, 1), p[2 * k + 1])
            for c in range(3):
                tq[2 * k, c, tg] = b0[c * 8 : c * 8 + 8]
                tq[2 * k + 1, c, tg] = b1[c * 8 : c * 8 + 8]
    x = [[tq[j, c, 2 * half : 2 * half + 2].reshape(16, 128) for j in range(4)] for c in range(3)]
    energy = [(x[0][j] * x[0][j] + x[1][j] * x[1][j] + x[2][j] * x[2][j]) * PROD for j in range(4)]
    g = lax.broadcasted_iota(jnp.int32, (16, 128), 0) % 8
    not_first, not_last = (g != 0).astype(f32), (g != 7).astype(f32)

    def box(values):
        flat = col_sum(values, masks)
        h = [flat[j * 16 : j * 16 + 16] for j in range(4)]
        above = [pltpu.roll(h[3], 1, 0) * not_first] + h[:3]
        below = h[1:] + [pltpu.roll(h[0], 15, 0) * not_last]
        return jnp.concatenate([h[j] + above[j] + below[j] for j in range(4)], 0)

    gains, _ = self_chain(jnp.concatenate(energy, 0), box)
    for layer in range(3):
        for j in range(4):
            gt[j, layer, 2 * half : 2 * half + 2] = gains[layer][j * 16 : j * 16 + 16].reshape(2, 8, 128)


def target_rows(ref, q, tg, first, count):
    return jnp.concatenate([ref[r % 4, q, tg, pl.ds(r // 4, 1), :][None] for r in range(first, first + count)], 0)


CHUNK = 8


def forward_unit(tg, srep, gsrep, tq, gt, xs, rs, hbuf, thacc, masks):
    def put(k, r0, value):
        hbuf[k, :, pl.ds(1 + r0, CHUNK)] = col_sum(value, masks)

    for r0 in range(0, 32, CHUNK):
        rows = pl.ds(r0, CHUNK)
        prod = srep[:, 0, rows] * target_rows(tq, 0, tg, r0, CHUNK)[None]
        prod += srep[:, 1, rows] * target_rows(tq, 1, tg, r0, CHUNK)[None]
        prod += srep[:, 2, rows] * target_rows(tq, 2, tg, r0, CHUNK)[None]
        put(0, r0, prod)
    total = None
    for layer in range(3):
        for r0 in range(0, 32, CHUNK):
            rows = pl.ds(r0, CHUNK)
            level = row_sum(hbuf, layer, r0) + BIAS_VAR
            x = level * gsrep[:, layer, rows] * target_rows(gt, layer, tg, r0, CHUNK)[None]
            rest = 1.0 - x * x
            root = lax.rsqrt(rest)
            xs[tg, :, layer, rows] = x
            rs[tg, :, layer, rows] = root
            value = x * horner(rest * root, NARROW if layer else WIDE, ALPHA if layer < 2 else BETA)
            if layer < 2:
                put(layer + 1, r0, value)
            else:
                part = jnp.sum(value, axis=1)
                total = part if total is None else total + part
    thacc[tg] = total


def row_sum(hbuf, k, r0):
    row = [hbuf[k, :, pl.ds(r0 + i, 1)] for i in range(CHUNK + 2)]
    sums = []
    for i in range(1, CHUNK + 1, 2):
        both = row[i] + row[i + 1]
        sums += [row[i - 1] + both, both + row[i + 2]]
    return jnp.concatenate(sums, 1)


def backward_unit(tg, gsrep, gt, xs, rs, vs, us, hbuf, masks):
    for layer in (2, 1, 0):
        for r0 in range(0, 32, CHUNK):
            rows = pl.ds(r0, CHUNK)
            d = rs[tg, :, layer, rows]
            if layer < 2:
                d = d * row_sum(hbuf, 1 - layer, r0)
            vs[tg, :, layer, rows] = d * xs[tg, :, layer, rows]
            d = d * gsrep[:, layer, rows] * target_rows(gt, layer, tg, r0, CHUNK)[None]
            hbuf[2 - layer, :, pl.ds(1 + r0, CHUNK)] = col_sum(d, masks)
    for r0 in range(0, 32, CHUNK):
        us[tg, :, pl.ds(r0, CHUNK)] = row_sum(hbuf, 2, r0)


def fold_rows(rows):
    block = lanes((1, 1, 128)) // 32
    r = (rows[1], rows[2], rows[3], rows[0])
    low, middle, odd = block < 2, (block == 1) | (block == 2), block % 2 == 1
    y0 = jnp.where(low, r[0], r[2]) + roll_lanes(jnp.where(low, r[2], r[0]), 64)
    y1 = jnp.where(middle, r[1], r[3]) + roll_lanes(jnp.where(middle, r[3], r[1]), 64)
    return jnp.where(odd, y0, y1) + roll_lanes(jnp.where(odd, y1, y0), 32)


def contract_rows(sg, cot, tq, vs, us, accs, nat):
    @pl.loop(0, 8, unroll=True)
    def _(g):
        for j in range(4):
            acc = [None] * 6
            for tg in range(4):
                weight = cot[tg]
                w = us[tg, sg, g * 4 + j] * weight
                terms = [w * tq[j, c, tg, pl.ds(g, 1), :] for c in range(3)]
                terms += [vs[tg, sg, layer, g * 4 + j] * weight for layer in range(3)]
                acc = [term if tg == 0 else old + term for old, term in zip(acc, terms)]
            for q in range(6):
                accs[q, j, g] = acc[q]

    for q in range(6):
        nat[sg, q] = fold_rows([accs[q, j] for j in range(4)])


def finish_supports(sg, nat, sbuf, slope_ref, gout, masks):
    def box(x):
        return box_natural(x[None], masks)[0]

    scale = (BETA * ALPHA * ALPHA, BETA * ALPHA, BETA)
    parts = [nat[sg, 3 + layer] * slope_ref[2 + layer, sg] * scale[layer] for layer in range(3)]
    d2 = parts[1] + box(parts[2]) * slope_ref[1, sg]
    d1 = parts[0] + box(d2) * slope_ref[0, sg]
    energy = box(d1) * (2.0 * PROD)
    for c in range(3):
        for g in range(8):
            at = pl.ds(sg * (8 * ROWS) + c * 8 + g, 8, stride=ROWS)
            gout[at, :] = nat[sg, c, g] * (BETA * ALPHA * ALPHA * PROD) + energy[g] * sbuf[at, :]


def split_dot(x, ones):
    high = x.astype(bf16)
    rest = x - high.astype(f32)
    middle = rest.astype(bf16)
    low = (rest - middle.astype(f32)).astype(bf16)
    dot = lambda part: jnp.dot(part, ones, preferred_element_type=f32)
    return dot(high) + dot(middle) + dot(low)


def kernel(
    sup_in, coef_in, tgt_in, lab_in, out_ref, res_ref,
    cin, lin, sbuf, tbuf, meta, meta2, thall, gout, gbuf,
    srep, gsrep, slope_ref, tq, gt, xs, rs, hbuf, thacc, vs, us, cot, accs, nat, expand, gather, spreadth,
    in_sem, ssend, tsend, csend, msend, thsend, gsend, srecv, trecv, krecv, crecv, mrecv, threcv, grecv,
):
    tgt, sup = lax.axis_index("tgt"), lax.axis_index("sup")
    z, xlo, core = sup // 4, (sup // 2) % 2, sup % 2
    a, b = xlo * 8 + tgt, z * 2 + core

    y, x = tgt // 2, (tgt % 2) * 2 + xlo

    def plane(dx, dy):
        to = (x + dx) % 4
        return (((y + dy) % 4) * 2 + to // 2, z * 4 + (to % 2) * 2 + core)

    def line(dz, dc):
        return (tgt, ((z + dz) % 8) * 4 + xlo * 2 + (core + dc) % 2)

    barrier = pltpu.get_barrier_semaphore()
    for near, far in zip(PLANE, LINE):
        pl.semaphore_signal(barrier, inc=1, device_id=plane(*near), device_id_type=MESH)
        pl.semaphore_signal(barrier, inc=1, device_id=line(*far), device_id_type=MESH)
    own = pl.multiple_of(a * ROWS, 8)
    mine = tbuf.at[b]
    slab = sbuf.at[pl.ds(own, ROWS)]
    loads = [
        pltpu.make_async_copy(src, dst, in_sem.at[i])
        for i, (src, dst) in enumerate(((sup_in, slab), (tgt_in, mine), (coef_in, cin), (lab_in, lin)))
    ]
    for load in loads:
        load.start()

    masks = col_masks()

    for load in loads:
        load.wait()
    fill = jnp.zeros((8, 128 - LABELS), f32)
    meta[b, 0:8, :] = jnp.concatenate([cin[...], fill], 1)
    meta[b, 8:9, :] = jnp.concatenate([lin[...], fill[:1]], 1)

    pl.semaphore_wait(barrier, 2 * (GROUP - 1))

    def send(src, dst, send_sem, recv_sem, device):
        copy = pltpu.make_async_remote_copy(
            src_ref=src, dst_ref=dst, send_sem=send_sem, recv_sem=recv_sem, device_id=device, device_id_type=MESH
        )
        copy.start()

    def all_arrived(ref, sem):
        pltpu.make_async_copy(ref, ref, sem).wait()

    sibling = (tgt, sup + 1 - 2 * core)
    order = (7, 1, 6, 2, 5, 3, 4)
    for i, d in enumerate(FAR_Z):
        send(mine, mine, tsend, trecv.at[d], line(d, 0))
        send(slab, slab, ssend, srecv, plane(*PLANE[2 * i]))
        send(slab, slab, ssend, srecv, plane(*PLANE[2 * i + 1]))
    send(slab, slab, ssend, srecv, plane(*PLANE[14]))
    send(mine, mine, tsend, krecv.at[0], sibling)

    def pass_on(steps, half):
        for d in steps:
            slot = tbuf.at[((z + 8 - d) % 8) * 2 + core]
            all_arrived(slot, trecv.at[d])
            send(slot, slot, tsend, krecv.at[half], sibling)

    def forward_half(half):
        @pl.loop(0, 2)
        def _(i):
            forward_unit(2 * half + i, srep, gsrep, tq, gt, xs, rs, hbuf, thacc, masks)

    hbuf[...] = jnp.zeros_like(hbuf)
    slots = [[((z + step + 8) % 8) * 2 + i for step in (-k, k + 1) for i in range(2)] for k in range(4)]

    def slot_of(place):
        unit, i = place // 4, place % 4
        return ((jnp.where(i < 2, -unit, unit + 1) + z + 8) % 8) * 2 + i % 2

    place = lax.broadcasted_iota(jnp.int32, (512, 128), 0) // 32
    gather[...] = (slot_of(place) == lanes((512, 128)) % 16).astype(f32).astype(bf16)
    place = lanes((128, 512)) // 32
    expand[...] = (slot_of(place) == lax.broadcasted_iota(jnp.int32, (128, 512), 0) % 16).astype(f32).astype(bf16)
    pass_on(order[:3], 0)
    all_arrived(tbuf.at[pl.ds(0, 4)], krecv.at[0])
    prepare_targets(0, slots, tbuf, tq, gt, masks)
    pass_on(order[3:], 1)
    others = sbuf.at[pl.ds(0, (GROUP - 1) * ROWS)]
    all_arrived(others, srecv)
    prepare_supports(sbuf, srep, gsrep, slope_ref, masks)
    for step in LINE:
        send(meta.at[b], meta.at[b], msend, mrecv, line(*step))
    forward_half(0)
    all_arrived(tbuf.at[pl.ds(0, 4)], krecv.at[1])
    prepare_targets(1, slots, tbuf, tq, gt, masks)
    forward_half(1)

    sums = jnp.concatenate(
        [jnp.concatenate([thacc[tg, sg] for tg in range(4)], 1) for sg in range(2)], 0
    )
    theta = split_dot(sums, gather[...]) + BIAS_VAR
    pick = (lax.broadcasted_iota(jnp.int32, (8, 128), 0) == lanes((8, 128)) // 16).astype(f32)
    for sg in range(2):
        thall[b, sg : sg + 1, :] = jnp.sum(theta[sg * 8 : sg * 8 + 8] * pick, axis=0, keepdims=True)
    for step in LINE:
        send(thall.at[b], thall.at[b], thsend, threcv, line(*step))

    all_arrived(meta.at[pl.ds(0, GROUP - 1)], mrecv)
    send(meta, meta2, csend, crecv, (tgt, z * 4 + (1 - xlo) * 2 + core))
    @pl.loop(0, 4)
    def _(tg):
        backward_unit(tg, gsrep, gt, xs, rs, vs, us, hbuf, masks)

    all_arrived(meta2, crecv)
    coeffs = jnp.concatenate([meta[b, 0:8, :], meta2[b, 0:8, :]], 0)
    coeffs_all = jnp.concatenate([ref[k, 0:8, :] for ref in (meta, meta2) for k in range(GROUP)], 0)
    labels = jnp.concatenate([meta[k, 8:9, :] for k in range(GROUP)], 0)
    contract_last = (((1,), (1,)), ((), ()))
    gram = lax.dot_general(coeffs, coeffs_all, contract_last, precision=HIGHEST, preferred_element_type=f32)
    wanted = lax.dot_general(coeffs, labels, contract_last, precision=HIGHEST, preferred_element_type=f32)
    wanted = jnp.concatenate([wanted, jnp.zeros((16, 112), f32)], 1)

    all_arrived(thall.at[pl.ds(0, GROUP - 1)], threcv)
    for other in range(2):
        for k in range(GROUP):
            spreadth[pl.ds(other * 128 + k * 8, 8), :] = thall[k, pl.ds((xlo + other) % 2, 1), :] * pick
    values = jnp.dot(gram, spreadth[...], precision=HIGHEST, preferred_element_type=f32) - wanted
    weights = split_dot(values, expand[...])
    for other in range(2):
        for tg in range(4):
            cot[tg, other] = weights[other * 8 : other * 8 + 8, tg * 128 : tg * 128 + 128]

    for other in range(2):
        sg = (xlo + other) % 2
        contract_rows(sg, cot[:, other], tq, vs, us, accs, nat)
        finish_supports(sg, nat, sbuf, slope_ref, gout, masks)
        for dx, dy in PLANE:
            if dx % 2 == other:
                to_tgt, to_sup = plane(dx, dy)
                piece = gout.at[pl.ds(pl.multiple_of((sg * 8 + to_tgt) * ROWS, 8), ROWS)]
                send(piece, gbuf.at[a], gsend, grecv, (to_tgt, to_sup))

    column = (lanes((1, 128)) % 16 == b).astype(f32)
    picked = jnp.sum(spreadth[...] * column, axis=1, keepdims=True)
    predicted = jnp.sum(picked * coeffs_all, axis=0, keepdims=True)
    res_ref[...] = (predicted - meta[b, 8:9, :])[:, :LABELS]

    gbuf[a] = gout[pl.ds(own, ROWS), :]
    all_arrived(gbuf.at[pl.ds(0, GROUP - 1)], grecv)
    total = gbuf[0]
    for k in range(1, GROUP):
        total = total + gbuf[k]
    out_ref[...] = total

    all_arrived(others, ssend)
    all_arrived(tbuf.at[pl.ds(0, GROUP - 1)], tsend)
    all_arrived(meta2, csend)
    all_arrived(meta.at[pl.ds(0, GROUP - 1)], msend)
    all_arrived(thall.at[pl.ds(0, GROUP - 1)], thsend)
    all_arrived(gbuf.at[pl.ds(0, GROUP - 1)], gsend)


def write(grad_in, res_in, grad_out, res_out, sem):
    copies = [
        pltpu.make_async_copy(src, dst, sem.at[i])
        for i, (src, dst) in enumerate(((grad_in, grad_out), (res_in, res_out)))
    ]
    for copy in copies:
        copy.start()
    for copy in copies:
        copy.wait()


def local(support, coeffs, targets, labels):
    vmem = lambda *shape: pltpu.VMEM(shape, f32)
    dma = pltpu.SemaphoreType.DMA
    grad, residual = pl.pallas_call(
        kernel,
        out_shape=(pltpu.VMEM((ROWS, 128), f32), pltpu.VMEM((1, LABELS), f32)),
        in_specs=[pl.BlockSpec(memory_space=pltpu.HBM)] * 4,
        out_specs=(pl.BlockSpec(memory_space=pltpu.VMEM), pl.BlockSpec(memory_space=pltpu.VMEM)),
        scratch_shapes=[
            vmem(8, LABELS), vmem(1, LABELS),
            vmem(GROUP * ROWS, 128), vmem(GROUP, ROWS, 128), vmem(GROUP, 9, 128), vmem(GROUP, 9, 128), vmem(GROUP, 2, 128),
            vmem(GROUP * ROWS, 128), vmem(GROUP, ROWS, 128),
            vmem(2, 3, 32, 8, 128), vmem(2, 3, 32, 8, 128), vmem(5, 2, 8, 8, 128),
            vmem(4, 3, 4, 8, 128), vmem(4, 3, 4, 8, 128),
            vmem(4, 2, 3, 32, 8, 128), vmem(4, 2, 3, 32, 8, 128), vmem(3, 2, 34, 8, 128), vmem(4, 2, 8, 128),
            vmem(4, 2, 3, 32, 8, 128), vmem(4, 2, 32, 8, 128), vmem(4, 2, 8, 128), vmem(6, 4, 8, 8, 128), vmem(2, 6, 8, 8, 128),
            pltpu.VMEM((128, 512), bf16), pltpu.VMEM((512, 128), bf16), vmem(256, 128),
            dma((4,)), dma, dma, dma, dma, dma, dma, dma, dma((8,)), dma((2,)), dma, dma, dma, dma,
        ],
        compiler_params=pltpu.CompilerParams(
            collective_id=0, has_side_effects=True, vmem_limit_bytes=56000 * 1024
        ),
    )(support.reshape(ROWS, 128), coeffs, targets.reshape(ROWS, 128), labels)
    grad, residual = pl.pallas_call(
        write,
        out_shape=(jax.ShapeDtypeStruct((ROWS, 128), f32), jax.ShapeDtypeStruct((1, LABELS), f32)),
        in_specs=[pl.BlockSpec(memory_space=pltpu.VMEM)] * 2,
        out_specs=(pl.BlockSpec(memory_space=pltpu.HBM), pl.BlockSpec(memory_space=pltpu.HBM)),
        scratch_shapes=[dma((2,))],
        compiler_params=pltpu.CompilerParams(vmem_limit_bytes=1024 * 1024),
    )(grad, residual)
    return grad.reshape(1, 3, 1024), residual


def solution(mesh):
    return jax.shard_map(
        local,
        mesh=mesh,
        in_specs=(
            P(("sup", "tgt"), None, None),
            P("sup", None),
            P(("tgt", "sup"), None, None),
            P(("tgt", "sup"), None),
        ),
        out_specs=(P(("sup", "tgt"), None, None), P(("tgt", "sup"), None)),
        check_vma=False,
    )
```

```python
import math

import jax
import jax.numpy as jnp
from jax import lax
from jax.experimental import pallas as pl
from jax.experimental.pallas import tpu as pltpu
from jax.sharding import PartitionSpec as P

f32 = jnp.float32
bf16 = jnp.bfloat16
MESH = pl.DeviceIdType.MESH
HIGHEST = lax.Precision.HIGHEST

WEIGHT_VAR = 1.6
BIAS_VAR = 0.1
LABELS = 100

GROUP = 16
ROWS = 24
SPREAD = WEIGHT_VAR / 9.0
PROD = SPREAD / 3.0
ALPHA = SPREAD * 2.0 / math.pi
BETA = WEIGHT_VAR / 1024.0 * 2.0 / math.pi

WIDE = (
    1.5707956460959935, -0.999909759045268, 0.7833927466035577, -0.6491778438734823, 0.5105887741390924,
    -0.3261364828462018, 0.1375277539431936, -0.027081268358035065,
)
NARROW = (1.5592713649848087, -0.9171235094499794, 0.5296910993035006, -0.21179670068297385, 0.039958000056267685)

PLANE = sorted(
    ((dx, dy) for dx in range(4) for dy in range(4) if dx or dy), key=lambda p: -min(p[0], 4 - p[0]) - min(p[1], 4 - p[1])
)
LINE = sorted(((dz, dc) for dz in range(8) for dc in range(2) if dz or dc), key=lambda p: -min(p[0], 8 - p[0]))
FAR_Z = (4, 5, 3, 6, 2, 7, 1)


def horner(w, coefs, scale):
    total = jnp.full_like(w, coefs[-1] * scale)
    for coef in coefs[-2::-1]:
        total = total * w + coef * scale
    return total


def lanes(shape):
    return lax.broadcasted_iota(jnp.int32, shape, len(shape) - 1)


def roll_lanes(x, shift):
    flat = x.reshape(-1, 128)
    return pltpu.roll(flat, shift, 1).reshape(x.shape)


def col_sum(x, masks):
    return x + roll_lanes(x, 1) * masks[0] + roll_lanes(x, 127) * masks[1]


def col_masks():
    col = lanes((1, 128)) % 32
    return (col != 0).astype(f32), (col != 31).astype(f32)


def self_chain(energy, box):
    gains, slopes = [], []
    level = box(energy) + BIAS_VAR
    for layer in range(3):
        gain = lax.rsqrt(1.0 + 2.0 * level)
        gains.append(gain)
        if layer < 2:
            square = gain * gain
            root = lax.rsqrt(1.0 + 4.0 * level)
            w = (1.0 + 4.0 * level) * root * square
            value = 2.0 * level * square * horner(w, NARROW if layer else WIDE, ALPHA)
            slopes.append((4.0 / math.pi * SPREAD) * square * root)
            level = box(value) + BIAS_VAR
    return gains, slopes


def box_natural(x, masks):
    h = col_sum(x, masks)
    lane = lanes((1, 1, 1, 128))
    zero = jnp.zeros_like(h[:, :1])
    above = roll_lanes(h, 32)
    below = roll_lanes(h, 96)
    above = jnp.where(lane < 32, jnp.concatenate([zero, above[:, :-1]], 1), above)
    below = jnp.where(lane >= 96, jnp.concatenate([below[:, 1:], zero], 1), below)
    return h + above + below


def prepare_supports(sbuf, srep, gsrep, slope_ref, masks):
    chans = [
        jnp.stack([sbuf[pl.ds(sg * 8 * ROWS + c * 8 + g, 8, stride=ROWS), :] for sg in range(2) for g in range(8)])
        for c in range(3)
    ]
    energy = (chans[0] * chans[0] + chans[1] * chans[1] + chans[2] * chans[2]) * PROD
    gains, slopes = self_chain(energy.reshape(2, 8, 8, 128), lambda x: box_natural(x, masks))
    for layer in range(2):
        slope_ref[layer] = slopes[layer]
    for layer in range(3):
        slope_ref[2 + layer] = -(gains[layer] * gains[layer])
    lane = lanes((1, 128))
    low, even = lane < 64, (lane // 32) % 2 == 0
    for q in range(6):
        src = chans[q] * PROD if q < 3 else gains[q - 3].reshape(16, 8, 128) * 2.0
        dst = srep if q < 3 else gsrep
        turned = roll_lanes(src, 64)
        first, second = jnp.where(low, src, turned), jnp.where(low, turned, src)
        t1, t2 = roll_lanes(first, 32), roll_lanes(second, 32)
        reps = (jnp.where(even, first, t1), jnp.where(even, t1, first), jnp.where(even, second, t2), jnp.where(even, t2, second))
        for j in range(4):
            for sg in range(2):
                for g in range(8):
                    dst[sg, q % 3, g * 4 + j] = reps[j][sg * 8 + g]


def prepare_targets(half, slots, tbuf, tq, gt, masks):
    lane = lanes((1, 128))
    low, even = lane < 64, (lane // 32) % 2 == 0
    for unit in range(2):
        tg = 2 * half + unit
        a = [tbuf[slots[tg][i]] for i in range(4)]
        p = [None] * 4
        for i in range(2):
            p[i] = jnp.where(low, a[i], pltpu.roll(a[i + 2], 64, 1))
            p[i + 2] = jnp.where(low, pltpu.roll(a[i], 64, 1), a[i + 2])
        for k in range(2):
            b0 = jnp.where(even, p[2 * k], pltpu.roll(p[2 * k + 1], 32, 1))
            b1 = jnp.where(even, pltpu.roll(p[2 * k], 96, 1), p[2 * k + 1])
            for c in range(3):
                tq[2 * k, c, tg] = b0[c * 8 : c * 8 + 8]
                tq[2 * k + 1, c, tg] = b1[c * 8 : c * 8 + 8]
    x = [[tq[j, c, 2 * half : 2 * half + 2].reshape(16, 128) for j in range(4)] for c in range(3)]
    energy = [(x[0][j] * x[0][j] + x[1][j] * x[1][j] + x[2][j] * x[2][j]) * PROD for j in range(4)]
    g = lax.broadcasted_iota(jnp.int32, (16, 128), 0) % 8
    not_first, not_last = (g != 0).astype(f32), (g != 7).astype(f32)

    def box(values):
        flat = col_sum(values, masks)
        h = [flat[j * 16 : j * 16 + 16] for j in range(4)]
        above = [pltpu.roll(h[3], 1, 0) * not_first] + h[:3]
        below = h[1:] + [pltpu.roll(h[0], 15, 0) * not_last]
        return jnp.concatenate([h[j] + above[j] + below[j] for j in range(4)], 0)

    gains, _ = self_chain(jnp.concatenate(energy, 0), box)
    for layer in range(3):
        for j in range(4):
            gt[j, layer, 2 * half : 2 * half + 2] = gains[layer][j * 16 : j * 16 + 16].reshape(2, 8, 128)


def target_rows(ref, q, tg, first, count):
    return jnp.concatenate([ref[r % 4, q, tg, pl.ds(r // 4, 1), :][None] for r in range(first, first + count)], 0)


CHUNK = 8


def forward_unit(tg, srep, gsrep, tq, gt, xs, rs, hbuf, thacc, masks):
    def put(k, r0, value):
        hbuf[k, :, pl.ds(1 + r0, CHUNK)] = col_sum(value, masks)

    for r0 in range(0, 32, CHUNK):
        rows = pl.ds(r0, CHUNK)
        prod = srep[:, 0, rows] * target_rows(tq, 0, tg, r0, CHUNK)[None]
        prod += srep[:, 1, rows] * target_rows(tq, 1, tg, r0, CHUNK)[None]
        prod += srep[:, 2, rows] * target_rows(tq, 2, tg, r0, CHUNK)[None]
        put(0, r0, prod)
    total = None
    for layer in range(3):
        for r0 in range(0, 32, CHUNK):
            rows = pl.ds(r0, CHUNK)
            level = row_sum(hbuf, layer, r0) + BIAS_VAR
            x = level * gsrep[:, layer, rows] * target_rows(gt, layer, tg, r0, CHUNK)[None]
            rest = 1.0 - x * x
            root = lax.rsqrt(rest)
            xs[tg, :, layer, rows] = x
            rs[tg, :, layer, rows] = root
            value = x * horner(rest * root, NARROW if layer else WIDE, ALPHA if layer < 2 else BETA)
            if layer < 2:
                put(layer + 1, r0, value)
            else:
                part = jnp.sum(value, axis=1)
                total = part if total is None else total + part
    thacc[tg] = total


def row_sum(hbuf, k, r0):
    row = [hbuf[k, :, pl.ds(r0 + i, 1)] for i in range(CHUNK + 2)]
    sums = []
    for i in range(1, CHUNK + 1, 2):
        both = row[i] + row[i + 1]
        sums += [row[i - 1] + both, both + row[i + 2]]
    return jnp.concatenate(sums, 1)


def backward_unit(tg, gsrep, gt, xs, rs, vs, us, hbuf, masks):
    for layer in (2, 1, 0):
        for r0 in range(0, 32, CHUNK):
            rows = pl.ds(r0, CHUNK)
            d = rs[tg, :, layer, rows]
            if layer < 2:
                d = d * row_sum(hbuf, 1 - layer, r0)
            vs[tg, :, layer, rows] = d * xs[tg, :, layer, rows]
            d = d * gsrep[:, layer, rows] * target_rows(gt, layer, tg, r0, CHUNK)[None]
            hbuf[2 - layer, :, pl.ds(1 + r0, CHUNK)] = col_sum(d, masks)
    for r0 in range(0, 32, CHUNK):
        us[tg, :, pl.ds(r0, CHUNK)] = row_sum(hbuf, 2, r0)


def fold_rows(rows):
    block = lanes((1, 1, 128)) // 32
    r = (rows[1], rows[2], rows[3], rows[0])
    low, middle, odd = block < 2, (block == 1) | (block == 2), block % 2 == 1
    y0 = jnp.where(low, r[0], r[2]) + roll_lanes(jnp.where(low, r[2], r[0]), 64)
    y1 = jnp.where(middle, r[1], r[3]) + roll_lanes(jnp.where(middle, r[3], r[1]), 64)
    return jnp.where(odd, y0, y1) + roll_lanes(jnp.where(odd, y1, y0), 32)


def contract_rows(sg, cot, tq, vs, us, accs, nat):
    @pl.loop(0, 8, unroll=True)
    def _(g):
        for j in range(4):
            acc = [None] * 6
            for tg in range(4):
                weight = cot[tg]
                w = us[tg, sg, g * 4 + j] * weight
                terms = [w * tq[j, c, tg, pl.ds(g, 1), :] for c in range(3)]
                terms += [vs[tg, sg, layer, g * 4 + j] * weight for layer in range(3)]
                acc = [term if tg == 0 else old + term for old, term in zip(acc, terms)]
            for q in range(6):
                accs[q, j, g] = acc[q]

    for q in range(6):
        nat[sg, q] = fold_rows([accs[q, j] for j in range(4)])


def finish_supports(sg, nat, sbuf, slope_ref, gout, masks):
    def box(x):
        return box_natural(x[None], masks)[0]

    scale = (BETA * ALPHA * ALPHA, BETA * ALPHA, BETA)
    parts = [nat[sg, 3 + layer] * slope_ref[2 + layer, sg] * scale[layer] for layer in range(3)]
    d2 = parts[1] + box(parts[2]) * slope_ref[1, sg]
    d1 = parts[0] + box(d2) * slope_ref[0, sg]
    energy = box(d1) * (2.0 * PROD)
    for c in range(3):
        for g in range(8):
            at = pl.ds(sg * (8 * ROWS) + c * 8 + g, 8, stride=ROWS)
            gout[at, :] = nat[sg, c, g] * (BETA * ALPHA * ALPHA * PROD) + energy[g] * sbuf[at, :]


def split_dot(x, ones):
    high = x.astype(bf16)
    rest = x - high.astype(f32)
    middle = rest.astype(bf16)
    low = (rest - middle.astype(f32)).astype(bf16)
    dot = lambda part: jnp.dot(part, ones, preferred_element_type=f32)
    return dot(high) + dot(middle) + dot(low)


def kernel(
    sup_in, coef_in, tgt_in, lab_in, out_ref, res_ref,
    cin, lin, sbuf, tbuf, meta, meta2, thall, gout, gbuf,
    srep, gsrep, slope_ref, tq, gt, xs, rs, hbuf, thacc, vs, us, cot, accs, nat, expand, gather, spreadth,
    in_sem, ssend, tsend, csend, msend, thsend, gsend, srecv, trecv, krecv, crecv, mrecv, threcv, grecv,
):
    tgt, sup = lax.axis_index("tgt"), lax.axis_index("sup")
    z, xlo, core = sup // 4, (sup // 2) % 2, sup % 2
    a, b = xlo * 8 + tgt, z * 2 + core

    y, x = tgt // 2, (tgt % 2) * 2 + xlo

    def plane(dx, dy):
        to = (x + dx) % 4
        return (((y + dy) % 4) * 2 + to // 2, z * 4 + (to % 2) * 2 + core)

    def line(dz, dc):
        return (tgt, ((z + dz) % 8) * 4 + xlo * 2 + (core + dc) % 2)

    barrier = pltpu.get_barrier_semaphore()
    for near, far in zip(PLANE, LINE):
        pl.semaphore_signal(barrier, inc=1, device_id=plane(*near), device_id_type=MESH)
        pl.semaphore_signal(barrier, inc=1, device_id=line(*far), device_id_type=MESH)
    own = pl.multiple_of(a * ROWS, 8)
    mine = tbuf.at[b]
    slab = sbuf.at[pl.ds(own, ROWS)]
    loads = [
        pltpu.make_async_copy(src, dst, in_sem.at[i])
        for i, (src, dst) in enumerate(((sup_in, slab), (tgt_in, mine), (coef_in, cin), (lab_in, lin)))
    ]
    for load in loads:
        load.start()

    masks = col_masks()

    for load in loads:
        load.wait()
    fill = jnp.zeros((8, 128 - LABELS), f32)
    meta[b, 0:8, :] = jnp.concatenate([cin[...], fill], 1)
    meta[b, 8:9, :] = jnp.concatenate([lin[...], fill[:1]], 1)

    pl.semaphore_wait(barrier, 2 * (GROUP - 1))

    def send(src, dst, send_sem, recv_sem, device):
        copy = pltpu.make_async_remote_copy(
            src_ref=src, dst_ref=dst, send_sem=send_sem, recv_sem=recv_sem, device_id=device, device_id_type=MESH
        )
        copy.start()

    def all_arrived(ref, sem):
        pltpu.make_async_copy(ref, ref, sem).wait()

    sibling = (tgt, sup + 1 - 2 * core)
    order = (7, 1, 6, 2, 5, 3, 4)
    for i, d in enumerate(FAR_Z):
        send(mine, mine, tsend, trecv.at[d], line(d, 0))
        send(slab, slab, ssend, srecv, plane(*PLANE[2 * i]))
        send(slab, slab, ssend, srecv, plane(*PLANE[2 * i + 1]))
    send(slab, slab, ssend, srecv, plane(*PLANE[14]))
    send(mine, mine, tsend, krecv.at[0], sibling)

    def pass_on(steps, half):
        for d in steps:
            slot = tbuf.at[((z + 8 - d) % 8) * 2 + core]
            all_arrived(slot, trecv.at[d])
            send(slot, slot, tsend, krecv.at[half], sibling)

    def forward_half(half):
        @pl.loop(0, 2, unroll=True)
        def _(i):
            forward_unit(2 * half + i, srep, gsrep, tq, gt, xs, rs, hbuf, thacc, masks)

    hbuf[...] = jnp.zeros_like(hbuf)
    slots = [[((z + step + 8) % 8) * 2 + i for step in (-k, k + 1) for i in range(2)] for k in range(4)]

    def slot_of(place):
        unit, i = place // 4, place % 4
        return ((jnp.where(i < 2, -unit, unit + 1) + z + 8) % 8) * 2 + i % 2

    place = lax.broadcasted_iota(jnp.int32, (512, 128), 0) // 32
    gather[...] = (slot_of(place) == lanes((512, 128)) % 16).astype(f32).astype(bf16)
    place = lanes((128, 512)) // 32
    expand[...] = (slot_of(place) == lax.broadcasted_iota(jnp.int32, (128, 512), 0) % 16).astype(f32).astype(bf16)
    pass_on(order[:3], 0)
    all_arrived(tbuf.at[pl.ds(0, 4)], krecv.at[0])
    prepare_targets(0, slots, tbuf, tq, gt, masks)
    pass_on(order[3:], 1)
    others = sbuf.at[pl.ds(0, (GROUP - 1) * ROWS)]
    all_arrived(others, srecv)
    prepare_supports(sbuf, srep, gsrep, slope_ref, masks)
    for step in LINE:
        send(meta.at[b], meta.at[b], msend, mrecv, line(*step))
    forward_half(0)
    all_arrived(tbuf.at[pl.ds(0, 4)], krecv.at[1])
    prepare_targets(1, slots, tbuf, tq, gt, masks)
    forward_half(1)

    sums = jnp.concatenate(
        [jnp.concatenate([thacc[tg, sg] for tg in range(4)], 1) for sg in range(2)], 0
    )
    theta = split_dot(sums, gather[...]) + BIAS_VAR
    pick = (lax.broadcasted_iota(jnp.int32, (8, 128), 0) == lanes((8, 128)) // 16).astype(f32)
    for sg in range(2):
        thall[b, sg : sg + 1, :] = jnp.sum(theta[sg * 8 : sg * 8 + 8] * pick, axis=0, keepdims=True)
    for step in LINE:
        send(thall.at[b], thall.at[b], thsend, threcv, line(*step))

    all_arrived(meta.at[pl.ds(0, GROUP - 1)], mrecv)
    send(meta, meta2, csend, crecv, (tgt, z * 4 + (1 - xlo) * 2 + core))
    @pl.loop(0, 4, unroll=True)
    def _(tg):
        backward_unit(tg, gsrep, gt, xs, rs, vs, us, hbuf, masks)

    all_arrived(meta2, crecv)
    coeffs = jnp.concatenate([meta[b, 0:8, :], meta2[b, 0:8, :]], 0)
    coeffs_all = jnp.concatenate([ref[k, 0:8, :] for ref in (meta, meta2) for k in range(GROUP)], 0)
    labels = jnp.concatenate([meta[k, 8:9, :] for k in range(GROUP)], 0)
    contract_last = (((1,), (1,)), ((), ()))
    gram = lax.dot_general(coeffs, coeffs_all, contract_last, precision=HIGHEST, preferred_element_type=f32)
    wanted = lax.dot_general(coeffs, labels, contract_last, precision=HIGHEST, preferred_element_type=f32)
    wanted = jnp.concatenate([wanted, jnp.zeros((16, 112), f32)], 1)

    all_arrived(thall.at[pl.ds(0, GROUP - 1)], threcv)
    for other in range(2):
        for k in range(GROUP):
            spreadth[pl.ds(other * 128 + k * 8, 8), :] = thall[k, pl.ds((xlo + other) % 2, 1), :] * pick
    values = jnp.dot(gram, spreadth[...], precision=HIGHEST, preferred_element_type=f32) - wanted
    weights = split_dot(values, expand[...])
    for other in range(2):
        for tg in range(4):
            cot[tg, other] = weights[other * 8 : other * 8 + 8, tg * 128 : tg * 128 + 128]

    for other in range(2):
        sg = (xlo + other) % 2
        contract_rows(sg, cot[:, other], tq, vs, us, accs, nat)
        finish_supports(sg, nat, sbuf, slope_ref, gout, masks)
        for dx, dy in PLANE:
            if dx % 2 == other:
                to_tgt, to_sup = plane(dx, dy)
                piece = gout.at[pl.ds(pl.multiple_of((sg * 8 + to_tgt) * ROWS, 8), ROWS)]
                send(piece, gbuf.at[a], gsend, grecv, (to_tgt, to_sup))

    column = (lanes((1, 128)) % 16 == b).astype(f32)
    picked = jnp.sum(spreadth[...] * column, axis=1, keepdims=True)
    predicted = jnp.sum(picked * coeffs_all, axis=0, keepdims=True)
    res_ref[...] = (predicted - meta[b, 8:9, :])[:, :LABELS]

    gbuf[a] = gout[pl.ds(own, ROWS), :]
    all_arrived(gbuf.at[pl.ds(0, GROUP - 1)], grecv)
    total = gbuf[0]
    for k in range(1, GROUP):
        total = total + gbuf[k]
    out_ref[...] = total

    all_arrived(others, ssend)
    all_arrived(tbuf.at[pl.ds(0, GROUP - 1)], tsend)
    all_arrived(meta2, csend)
    all_arrived(meta.at[pl.ds(0, GROUP - 1)], msend)
    all_arrived(thall.at[pl.ds(0, GROUP - 1)], thsend)
    all_arrived(gbuf.at[pl.ds(0, GROUP - 1)], gsend)


def write(grad_in, res_in, grad_out, res_out, sem):
    copies = [
        pltpu.make_async_copy(src, dst, sem.at[i])
        for i, (src, dst) in enumerate(((grad_in, grad_out), (res_in, res_out)))
    ]
    for copy in copies:
        copy.start()
    for copy in copies:
        copy.wait()


def local(support, coeffs, targets, labels):
    vmem = lambda *shape: pltpu.VMEM(shape, f32)
    dma = pltpu.SemaphoreType.DMA
    grad, residual = pl.pallas_call(
        kernel,
        out_shape=(pltpu.VMEM((ROWS, 128), f32), pltpu.VMEM((1, LABELS), f32)),
        in_specs=[pl.BlockSpec(memory_space=pltpu.HBM)] * 4,
        out_specs=(pl.BlockSpec(memory_space=pltpu.VMEM), pl.BlockSpec(memory_space=pltpu.VMEM)),
        scratch_shapes=[
            vmem(8, LABELS), vmem(1, LABELS),
            vmem(GROUP * ROWS, 128), vmem(GROUP, ROWS, 128), vmem(GROUP, 9, 128), vmem(GROUP, 9, 128), vmem(GROUP, 2, 128),
            vmem(GROUP * ROWS, 128), vmem(GROUP, ROWS, 128),
            vmem(2, 3, 32, 8, 128), vmem(2, 3, 32, 8, 128), vmem(5, 2, 8, 8, 128),
            vmem(4, 3, 4, 8, 128), vmem(4, 3, 4, 8, 128),
            vmem(4, 2, 3, 32, 8, 128), vmem(4, 2, 3, 32, 8, 128), vmem(3, 2, 34, 8, 128), vmem(4, 2, 8, 128),
            vmem(4, 2, 3, 32, 8, 128), vmem(4, 2, 32, 8, 128), vmem(4, 2, 8, 128), vmem(6, 4, 8, 8, 128), vmem(2, 6, 8, 8, 128),
            pltpu.VMEM((128, 512), bf16), pltpu.VMEM((512, 128), bf16), vmem(256, 128),
            dma((4,)), dma, dma, dma, dma, dma, dma, dma, dma((8,)), dma((2,)), dma, dma, dma, dma,
        ],
        compiler_params=pltpu.CompilerParams(
            collective_id=0, has_side_effects=True, vmem_limit_bytes=56000 * 1024
        ),
    )(support.reshape(ROWS, 128), coeffs, targets.reshape(ROWS, 128), labels)
    grad, residual = pl.pallas_call(
        write,
        out_shape=(jax.ShapeDtypeStruct((ROWS, 128), f32), jax.ShapeDtypeStruct((1, LABELS), f32)),
        in_specs=[pl.BlockSpec(memory_space=pltpu.VMEM)] * 2,
        out_specs=(pl.BlockSpec(memory_space=pltpu.HBM), pl.BlockSpec(memory_space=pltpu.HBM)),
        scratch_shapes=[dma((2,))],
        compiler_params=pltpu.CompilerParams(vmem_limit_bytes=1024 * 1024),
    )(grad, residual)
    return grad.reshape(1, 3, 1024), residual


def solution(mesh):
    return jax.shard_map(
        local,
        mesh=mesh,
        in_specs=(
            P(("sup", "tgt"), None, None),
            P("sup", None),
            P(("tgt", "sup"), None, None),
            P(("tgt", "sup"), None),
        ),
        out_specs=(P(("sup", "tgt"), None, None), P(("tgt", "sup"), None)),
        check_vma=False,
    )
```
